256 devices in a mesh: replica: 8 (over z_lo, x), fsdp: 32 (over y, z_hi, core).
Axes of the slice: x: 4, y: 4, z: 8 (z_hi: 4, z_lo: 2; z = z_hi * 2 + z_lo), core: 2. Of those that a mesh axis runs over, the one named last changes fastest.
Arguments:
- tokens: bfloat16 [8, 8192, 8192], P('replica', 'fsdp'), may hold values from -6 to 6
- queries: bfloat16 [8, 8192, 4096], P('replica', 'fsdp'), may hold values from -480 to 480
- segments: int32 [8, 32, 256], P('replica', 'fsdp'), may hold values from 0 to 7, never falling along the last dimension, each value on 1 to 128 neighbouring positions
- local_weights: bfloat16 [8, 8192, 1024], P('replica', 'fsdp'), may hold values from -6 to 6
- global_params: float32 [8192, 1024], P('fsdp'), may hold values from -6 to 6
- momentum: float32 [8192, 1024], P('fsdp'), may hold values from -6 to 6
Outputs:
- attended: bfloat16 [8, 8192, 4096], P('replica', 'fsdp')
- new_params: float32 [8192, 1024], P('fsdp')
- new_momentum: float32 [8192, 1024], P('fsdp')
The draws below stay inside these ranges and needn't reach their ends.
Inputs may be any that keep to these rules, and one draw needn't show every extreme that they name: `segments`: document numbers never fall along a sequence; each document has 1 to 128 positions and one has exactly 128.
All inputs are finite; a program needn't handle non-finite values.
Results may differ from the reference program's by a relative error of at most 0.012.
The reference program's roundings to bfloat16 on the way (of `pairs` and `probs`) count: a program that leaves them out, or rounds other values in their place, can miss the bound.
Values may be sent and summed in bfloat16 or wider, within the bound.
A program may use at most 128 MiB of HBM per device.

```python
import math
import jax
import jax.numpy as jnp
import numpy as np
from jax import lax

D = 8192
HD = 128
HEADS_KV = 4
Q_GROUP = 8
DOCS = 8
TOK_DEV = 256
MOST = 128
QH = 32
KVW = 1024
REPLICAS = 8
SEQS = 32
TOKENS = 8192


def draw_queries(key, part):
    key = jax.random.fold_in(key, 11)
    base_key = jax.random.fold_in(key, 0)
    values = jnp.clip(jax.random.normal(base_key, (REPLICAS, TOKENS, QH * HD), jnp.float32), -6.0, 6.0)
    return values.astype(jnp.bfloat16)


def shard_levels(own_key, dims, cuts, smallest, largest):
    def one(axis_at, shards_of):
        draws = jax.random.uniform(jax.random.fold_in(jax.random.fold_in(own_key, 6), axis_at), (shards_of,), jnp.float32, smallest / len(cuts), largest / len(cuts))
        return jnp.repeat(jnp.exp(draws), dims[axis_at] // shards_of).reshape((-1,) + (1,) * (len(dims) - axis_at - 1))

    loudness = one(*cuts[0])
    for cut in cuts[1:]:
        loudness = loudness * one(*cut)
    return loudness


def split_up(amount, total, bound, lean):
    loads = [(1 << 20) // math.isqrt(standing ** lean) + 1 for standing in range(2, amount + 1)]
    spare, holding = total - bound - (amount - 1), [1] * (amount - 1)
    while spare > 0:
        movable = [i for i in range(amount - 1) if holding[i] < bound]
        mass, remaining = sum([loads[i] for i in movable]), spare
        for i in movable:
            extra = min(bound - holding[i], max(1, remaining * loads[i] // mass), spare)
            holding[i] = holding[i] + extra
            spare = spare - extra
    return np.array([bound] + holding)


def ragged(stream_key, count, total, reach, lean):
    if count == 2:
        one = jax.random.randint(stream_key, (), max(1, total - reach), min(reach, total - 1) + 1)
        return jnp.stack([one, total - one])
    tallies = jnp.asarray(split_up(count, total, reach, lean), jnp.int32)
    couples = (count - 1) // 2
    source_of, sink = tallies[1:1 + 2 * couples:2], tallies[2:2 + 2 * couples:2]
    slack = jnp.minimum(source_of - 1, reach - sink)
    passed = jax.random.randint(jax.random.fold_in(stream_key, 1), (couples,), 0, 1 << 20) % (slack + 1)
    tallies = tallies.at[1:1 + 2 * couples:2].set(source_of - passed).at[2:2 + 2 * couples:2].set(sink + passed)
    return tallies[jax.random.permutation(jax.random.fold_in(stream_key, 2), count)]


def bell_draw(stream_key, extent, spread, reach, cuts=(), kind=jnp.bfloat16):
    level = shard_levels(stream_key, extent, cuts, -0.22, 0.18) if cuts else 1.0
    drawn = jax.random.normal(stream_key, extent, jnp.float32) * spread * level
    return jnp.minimum(jnp.maximum(drawn, -reach), reach).astype(kind)


def setup_inputs(seed: int = 0) -> dict:
    key_of = jax.random.split(jax.random.key(seed), 7)
    return {
        "tokens": bell_draw(key_of[0], (REPLICAS, TOKENS, D), 1.0, 6.0, ((0, 8), (1, 32))),
        "queries": draw_queries(jax.random.fold_in(key_of[6], 71), 0),
        "segments": jax.vmap(lambda own: jnp.searchsorted(jnp.cumsum(ragged(own, DOCS, TOK_DEV, MOST, 2)), jnp.arange(TOK_DEV), side="right"))(jax.random.split(key_of[2], REPLICAS * SEQS)).reshape((REPLICAS, SEQS, TOK_DEV)).astype(jnp.int32),
        "local_weights": bell_draw(key_of[3], (REPLICAS, D, KVW), 1.0, 6.0, ((0, 8), (1, 32))),
        "global_params": bell_draw(key_of[4], (D, KVW), 1.0, 6.0, ((0, 32),), jnp.float32),
        "momentum": bell_draw(key_of[5], (D, KVW), 1.0, 6.0, ((0, 32),), jnp.float32),
    }


def attend(args):
    query, pairs, ids = args
    length = query.shape[0]
    keys = pairs[:, :HEADS_KV * HD].reshape(length, HEADS_KV, HD).astype(jnp.float32)
    values = pairs[:, HEADS_KV * HD:].reshape(length, HEADS_KV, HD).astype(jnp.float32)
    query_heads = query.reshape(length, HEADS_KV, Q_GROUP, HD).astype(jnp.float32)
    scores = jnp.einsum("thgd,shd->hgts", query_heads, keys) * (HD ** -0.5)
    position = jnp.arange(length, dtype=jnp.int32)
    allowed = (ids[:, None] == ids[None, :]) & (position[None, :] <= position[:, None])
    scores = jnp.where(allowed, scores, -jnp.inf)
    row_max = jnp.max(scores, axis=-1, keepdims=True)
    weights = jnp.exp(scores - row_max)
    probs = (weights / jnp.sum(weights, axis=-1, keepdims=True)).astype(jnp.bfloat16)
    mixed = jnp.einsum("hgts,shd->thgd", probs.astype(jnp.float32), values)
    return mixed.reshape(length, QH * HD).astype(jnp.bfloat16)


def one_replica(args):
    features, query, ids, weights = args
    pairs = (jnp.dot(features, weights, preferred_element_type=jnp.float32) * (D ** -0.5)).astype(jnp.bfloat16)
    pairs = pairs.reshape(SEQS, TOK_DEV, KVW)
    query = query.reshape(SEQS, TOK_DEV, QH * HD)
    mixed = lax.map(attend, (query, pairs, ids))
    return mixed.reshape(TOKENS, QH * HD)


def reference(tokens, queries, segments, local_weights, global_params, momentum):
    attended = lax.map(one_replica, (tokens, queries, segments, local_weights))
    delta = global_params[None] - local_weights.astype(jnp.float32)
    outer_grad = jnp.sum(delta, axis=0) / REPLICAS
    new_momentum = 0.9 * momentum + outer_grad
    new_params = global_params - 0.7 * (outer_grad + 0.9 * new_momentum)
    return attended, new_params, new_momentum
```

```python
import math

import jax
import jax.numpy as jnp
from jax import lax
from jax.experimental import pallas as pl
from jax.experimental.pallas import tpu as pltpu
from jax.sharding import PartitionSpec as P

HD = 128
QH = 32
Q_GROUP = 8
ROWS = 256
WIDTH = 8192
KVW = 1024
BLK = 256
NQ = KVW // BLK
CHIPS = 16
X = 4
PART = ROWS // X
MESH = pl.DeviceIdType.MESH

NODES = (
    (0, 1), (0, -1), (1, 0), (-1, 0), (2, 0),
    (1, 1), (-1, 1), (1, -1), (-1, -1), (0, 2),
    (2, 1), (2, -1), (1, 2), (-1, 2), (2, 2),
)
TREE = {
    (0, 0): ((0, 1), (0, -1), (1, 0), (-1, 0)),
    (0, 1): ((0, 2), (1, 1), (-1, 1)),
    (0, -1): ((1, -1), (-1, -1)),
    (1, 0): ((2, 0),),
    (1, 1): ((1, 2),),
    (-1, 1): ((2, 1),),
    (1, -1): ((2, -1),),
    (-1, -1): ((-1, 2),),
    (-1, 2): ((2, 2),),
}
PARENT = {child: node for node, children in TREE.items() for child in children}
ORDER = (
    -18, -34, -2, -19, -16, -49, -33, -47, -17, -1, 17, -32, -4, 1, 15,
    7, 19, 16, 0, 46, -3, 21, 8, 11, 22, 18, 23, 31, 20, -46,
    28, 38, 3, 32, 33, 13, 2, 5, 24, 29, 26, 9, 6, 25, -31,
    45, 53, -48, 27, 48, 43, 4, 12, 10, 14, 50, 30, 47, 51, 37,
    44, 58, 52, 36, 35, 49, 54, 41, 57, 34, 39, 59, 55, 56, 40,
    42,
)
GROUP = 4
RECEIVES = [code for code in ORDER if code >= 0]
SUM_AT, SPREAD_AT, UPDATE_AT = 10, 36, 52


def kernel(
    tokens, queries, segs, weights, params, moment,
    attended, new_params, new_moment,
    gathered, feats, acc, incoming, qv, bias, probs, keys, mixed,
    raw, partsum, partin, total, gv, mv,
    gsend, grecv, tsend, trecv, xsend, xrecv, zsend, zrecv, bsend, brecv, psend, precv,
    own_sem, feat_sem, q_sem, raw_sem, g_sem, m_sem, o_sem, np_sem, nm_sem,
):
    r = lax.axis_index("replica")
    f = lax.axis_index("fsdp")
    zl, x = r // X, r % X
    y, zh, c = f // 8, (f // 2) % 4, f % 2
    sign = 1 - 2 * c
    other = 1 - c
    sibling = (r, f + 1 - 2 * c)
    zpeer = ((1 - zl) * X + x, f)

    def xpeer(step):
        return (zl * X + (x + step) % X, f)

    def dev(dy, dz):
        return (r, (((y + dy + 4) % 4) * 4 + (zh + dz * sign + 4) % 4) * 2 + c)

    def slot(node):
        return ((y - node[0] + 4) % 4) * 4 + (zh - node[1] * sign + 4) % 4

    own = y * 4 + zh

    own_feats = [
        pltpu.make_async_copy(
            tokens.at[:, pl.ds(pl.multiple_of((2 * o + c) * BLK, BLK), BLK)],
            feats.at[o, pl.ds(pl.multiple_of(c * ROWS, ROWS), ROWS)],
            feat_sem,
        )
        for o in range(CHIPS)
    ]
    own_weights = [
        pltpu.make_async_copy(weights.at[:, pl.ds(q * BLK, BLK)], gathered.at[own, q], own_sem.at[q])
        for q in range(NQ)
    ]
    q_copy = pltpu.make_async_copy(queries, qv, q_sem)
    g_copy = pltpu.make_async_copy(params, gv, g_sem)
    m_copy = pltpu.make_async_copy(moment, mv, m_sem)
    raw_copy = pltpu.make_async_copy(weights.at[pl.ds(pl.multiple_of(x * PART, PART), PART)], raw.at[x], raw_sem)

    barrier = pltpu.get_barrier_semaphore()
    peers = [dev(1, 0), dev(-1, 0), dev(0, 1), dev(0, -1), sibling, zpeer, xpeer(1), xpeer(2), xpeer(3)]
    for peer in peers:
        pl.semaphore_signal(barrier, inc=1, device_id=peer, device_id_type=MESH)
    for copy in own_weights + own_feats:
        copy.start()
    raw_copy.start()
    pl.semaphore_wait(barrier, len(peers))

    def hop(q, child):
        node = PARENT[child]
        at, index = slot(node), NODES.index(child)
        source = weights.at[:, pl.ds(q * BLK, BLK)] if node == (0, 0) else gathered.at[at, q]
        return pltpu.make_async_remote_copy(
            src_ref=source, dst_ref=gathered.at[at, q],
            send_sem=gsend.at[q, index], recv_sem=grecv.at[q, index],
            device_id=dev(*step_of(child)), device_id_type=MESH,
        )

    def step_of(child):
        node = PARENT[child]
        dy, dz = (child[0] - node[0]) % 4, (child[1] - node[1]) % 4
        return (dy - 4 if dy == 3 else dy, dz - 4 if dz == 3 else dz)

    def arrive(q, node):
        at, index = slot(node), NODES.index(node)
        pltpu.make_async_remote_copy(
            src_ref=gathered.at[at, q], dst_ref=gathered.at[at, q],
            send_sem=gsend.at[q, index], recv_sem=grecv.at[q, index],
            device_id=sibling, device_id_type=MESH,
        ).wait_recv()

    def feat_send(o):
        return pltpu.make_async_remote_copy(
            src_ref=tokens.at[:, pl.ds(pl.multiple_of((2 * o + other) * BLK, BLK), BLK)],
            dst_ref=feats.at[o, pl.ds(pl.multiple_of(c * ROWS, ROWS), ROWS)],
            send_sem=tsend, recv_sem=trecv, device_id=sibling, device_id_type=MESH,
        )

    def all_feats(row_core):
        view = feats.at[:, pl.ds(pl.multiple_of(row_core * ROWS, ROWS), ROWS)]
        return pltpu.make_async_remote_copy(
            src_ref=view, dst_ref=view, send_sem=tsend, recv_sem=trecv, device_id=sibling, device_id_type=MESH
        )

    def raw_send(step):
        to = (x + step) % X
        return pltpu.make_async_remote_copy(
            src_ref=weights.at[pl.ds(pl.multiple_of(to * PART, PART), PART)], dst_ref=raw.at[x],
            send_sem=xsend.at[step - 1], recv_sem=xrecv.at[step - 1], device_id=xpeer(step), device_id_type=MESH,
        )

    def raw_arrive(step):
        at = (x - step + X) % X
        pltpu.make_async_remote_copy(
            src_ref=raw.at[at], dst_ref=raw.at[at],
            send_sem=xsend.at[step - 1], recv_sem=xrecv.at[step - 1], device_id=xpeer(step), device_id_type=MESH,
        ).wait_recv()

    z_copy = pltpu.make_async_remote_copy(
        src_ref=partsum, dst_ref=partin, send_sem=zsend, recv_sem=zrecv, device_id=zpeer, device_id_type=MESH
    )

    def spread(step):
        return pltpu.make_async_remote_copy(
            src_ref=total.at[x], dst_ref=total.at[x],
            send_sem=bsend.at[step - 1], recv_sem=brecv.at[step - 1], device_id=xpeer(step), device_id_type=MESH,
        )

    def spread_arrive(step):
        at = (x - step + X) % X
        pltpu.make_async_remote_copy(
            src_ref=total.at[at], dst_ref=total.at[at],
            send_sem=bsend.at[step - 1], recv_sem=brecv.at[step - 1], device_id=xpeer(step), device_id_type=MESH,
        ).wait_recv()

    def exchange(q):
        return pltpu.make_async_remote_copy(
            src_ref=acc.at[q, pl.ds(pl.multiple_of(other * ROWS, ROWS), ROWS)], dst_ref=incoming.at[q],
            send_sem=psend.at[q], recv_sem=precv.at[q], device_id=sibling, device_id_type=MESH,
        )

    def multiply(q, nodes, fresh=False):
        slots = [slot(node) for node in nodes]

        @pl.loop(0, 2)
        def _(half):
            at = pl.ds(pl.multiple_of(half * ROWS, ROWS), ROWS)
            partial = None
            for s in slots:
                term = jnp.dot(feats[s, at, :], gathered[s, q], preferred_element_type=jnp.float32)
                partial = term if partial is None else partial + term
            acc[q, at, :] = partial if fresh else acc[q, at, :] + partial

    def finish_block(q):
        mine = acc[q, pl.ds(pl.multiple_of(c * ROWS, ROWS), ROWS), :]
        return ((mine + incoming[q]) * WIDTH ** (-0.5)).astype(jnp.bfloat16)

    def softmax_heads(start):
        kv = start // Q_GROUP

        @pl.loop(0, 2)
        def _(i):
            h = start + i
            head = qv[:, pl.ds(pl.multiple_of(h * HD, HD), HD)]
            scores = lax.dot_general(
                head, keys[:, kv * HD : (kv + 1) * HD], (((1,), (1,)), ((), ())), preferred_element_type=jnp.float32
            )
            scores = scores * (HD ** (-0.5) * math.log2(math.e)) + bias[...]
            top = jnp.max(scores, axis=1, keepdims=True)
            weight = jnp.exp2(scores - top)
            norm = 1.0 / jnp.sum(weight, axis=1, keepdims=True)
            probs[h] = (weight * norm).astype(jnp.bfloat16)

    def mix(q):
        first = (q - 2) * 2 * Q_GROUP
        block = finish_block(q)
        for j in range(2):
            values = block[:, j * HD : (j + 1) * HD]
            base = first + j * Q_GROUP

            @pl.loop(0, Q_GROUP)
            def _(i):
                h = base + i
                out = jnp.dot(probs[h], values, preferred_element_type=jnp.float32)
                mixed[:, pl.ds(pl.multiple_of(h * HD, HD), HD)] = out.astype(jnp.bfloat16)

        return pltpu.make_async_copy(
            mixed.at[:, pl.ds(first * HD, 2 * Q_GROUP * HD)], attended.at[:, pl.ds(first * HD, 2 * Q_GROUP * HD)],
            o_sem.at[q - 2],
        )

    def sum_raw():
        for step in (1, 2, 3):
            raw_arrive(step)
        raw_copy.wait()
        partsum[...] = (
            raw[0].astype(jnp.float32) + raw[1].astype(jnp.float32) + raw[2].astype(jnp.float32) + raw[3].astype(jnp.float32)
        )
        z_copy.start()

    def spread_total():
        z_copy.wait()
        total[x] = partsum[...] + partin[...]
        for step in (1, 2, 3):
            spread(step).start()

    np_copy = pltpu.make_async_copy(gv, new_params, np_sem)
    nm_copy = pltpu.make_async_copy(mv, new_moment, nm_sem)

    def update():
        for step in (1, 2, 3):
            spread_arrive(step)
        g_copy.wait()
        m_copy.wait()

        @pl.loop(0, X)
        def _(j):
            at = pl.ds(pl.multiple_of(j * PART, PART), PART)
            g = gv[at, :]
            grad = g - total[j] * 0.125
            fresh = 0.9 * mv[at, :] + grad
            mv[at, :] = fresh
            gv[at, :] = g - 0.7 * (grad + 0.9 * fresh)

        np_copy.start()
        nm_copy.start()

    pending = {q: [] for q in range(NQ)}
    left = {q: CHIPS - 1 for q in range(NQ)}
    started = set()
    todo = []
    state = {"ready": False, "queries": False}

    def flush(q):
        if pending[q]:
            multiply(q, pending[q], fresh=q not in started)
            started.add(q)
            pending[q] = []

    outs = []

    def settle(q):
        exchange(q).wait_recv()
        if q < 2:
            keys[:, q * BLK : (q + 1) * BLK] = finish_block(q)
            if not state["queries"]:
                state["queries"] = True
                q_copy.wait()
            todo.extend(range(q * 2 * Q_GROUP, (q + 1) * 2 * Q_GROUP, 2))
        else:
            copy = mix(q)
            copy.start()
            outs.append(copy)

    waiting = []
    done = 0
    opened = False
    for code in ORDER:
        if code < 0:
            q, n = divmod(-code - 1, 15)
            hop(q, NODES[n]).start()
            continue
        if not opened:
            opened = True
            for step in (1, 2, 3):
                raw_send(step).start()
            for o in range(CHIPS):
                feat_send(o).start()
            q_copy.start()
            g_copy.start()
            m_copy.start()
            row = lax.broadcast_in_dim(segs[...], (ROWS, ROWS), (0, 1))
            t_at = lax.broadcasted_iota(jnp.int32, (ROWS, ROWS), 0)
            s_at = lax.broadcasted_iota(jnp.int32, (ROWS, ROWS), 1)
            allowed = (row == row.T) & (s_at <= t_at)
            bias[...] = jnp.where(allowed, 0.0, -1e30)
        q, n = divmod(code, 15)
        arrive(q, NODES[n])
        for child in TREE.get(NODES[n], ()):
            hop(q, child).start()
        done += 1
        pending[q].append(NODES[n])
        left[q] -= 1
        if not state["ready"] and done >= 4:
            state["ready"] = True
            for o in own_weights:
                o.wait()
            view = feats.at[:, pl.ds(pl.multiple_of(c * ROWS, ROWS), ROWS)]
            pltpu.make_async_copy(view, view, feat_sem).wait()
            all_feats(other).wait_recv()
            for qq in range(NQ):
                pending[qq].append((0, 0))
        if state["ready"] and (len(pending[q]) >= GROUP or left[q] == 0):
            flush(q)
        for item in list(waiting):
            if done >= item[0] + 2 and (item[1] < 2 or not todo):
                waiting.remove(item)
                settle(item[1])
        if left[q] == 0:
            exchange(q).start()
            waiting.append((done, q))
        if done == SUM_AT:
            sum_raw()
        if done == SPREAD_AT:
            spread_total()
        if done == UPDATE_AT:
            update()
        remaining = len(RECEIVES) - done
        if todo:
            count = -(-len(todo) // max(1, remaining - 3))
            for start in todo[:count]:
                softmax_heads(start)
            del todo[:count]

    for start in todo:
        softmax_heads(start)
    for _, q in waiting:
        settle(q)

    for q in range(NQ):
        for child in NODES:
            hop(q, child).wait_send()
        exchange(q).wait_send()
    all_feats(other).wait_send()
    for step in (1, 2, 3):
        raw_send(step).wait_send()
        spread(step).wait_send()
    np_copy.wait()
    nm_copy.wait()
    for copy in outs:
        copy.wait()


def shards(tokens, queries, segments, local_weights, global_params, momentum):
    any_space = pl.BlockSpec(memory_space=pl.ANY)
    vmem = pl.BlockSpec(memory_space=pltpu.VMEM)
    dma = pltpu.SemaphoreType.DMA
    attended, new_params, new_momentum = pl.pallas_call(
        kernel,
        out_shape=(
            jax.ShapeDtypeStruct((ROWS, QH * HD), jnp.bfloat16),
            jax.ShapeDtypeStruct((ROWS, KVW), jnp.float32),
            jax.ShapeDtypeStruct((ROWS, KVW), jnp.float32),
        ),
        in_specs=[any_space, any_space, vmem, any_space, any_space, any_space],
        out_specs=(any_space, any_space, any_space),
        scratch_shapes=[
            pltpu.VMEM((CHIPS, NQ, BLK, BLK), jnp.bfloat16),
            pltpu.VMEM((CHIPS, 2 * ROWS, BLK), jnp.bfloat16),
            pltpu.VMEM((NQ, 2 * ROWS, BLK), jnp.float32),
            pltpu.VMEM((NQ, ROWS, BLK), jnp.float32),
            pltpu.VMEM((ROWS, QH * HD), jnp.bfloat16),
            pltpu.VMEM((ROWS, ROWS), jnp.float32),
            pltpu.VMEM((QH, ROWS, ROWS), jnp.bfloat16),
            pltpu.VMEM((ROWS, 2 * BLK), jnp.bfloat16),
            pltpu.VMEM((ROWS, QH * HD), jnp.bfloat16),
            pltpu.VMEM((X, PART, KVW), jnp.bfloat16),
            pltpu.VMEM((PART, KVW), jnp.float32),
            pltpu.VMEM((PART, KVW), jnp.float32),
            pltpu.VMEM((X, PART, KVW), jnp.float32),
            pltpu.VMEM((ROWS, KVW), jnp.float32),
            pltpu.VMEM((ROWS, KVW), jnp.float32),
            dma((NQ, 15)), dma((NQ, 15)), dma, dma, dma((3,)), dma((3,)), dma, dma, dma((3,)), dma((3,)),
            dma((NQ,)), dma((NQ,)),
            dma((NQ,)), dma, dma, dma, dma, dma, dma((2,)), dma, dma,
        ],
        compiler_params=pltpu.CompilerParams(
            collective_id=0, has_side_effects=True, vmem_limit_bytes=56 * 2**20
        ),
        cost_estimate=pl.CostEstimate(flops=6 * 10**9, bytes_accessed=13 * 2**20, transcendentals=2**21),
        name="sync_and_attend",
    )(tokens[0], queries[0], segments[0], local_weights[0], global_params, momentum)
    return (attended[None], new_params, new_momentum)


def solution(mesh):
    placed = (
        P("replica", "fsdp", None),
        P("replica", "fsdp", None),
        P("replica", "fsdp", None),
        P("replica", "fsdp", None),
        P("fsdp", None),
        P("fsdp", None),
    )
    return jax.shard_map(
        shards,
        mesh=mesh,
        in_specs=placed,
        out_specs=(P("replica", "fsdp", None), P("fsdp", None), P("fsdp", None)),
        check_vma=False,
    )
```

```python
import math

import jax
import jax.numpy as jnp
from jax import lax
from jax.experimental import pallas as pl
from jax.experimental.pallas import tpu as pltpu
from jax.sharding import PartitionSpec as P

HD = 128
QH = 32
Q_GROUP = 8
ROWS = 256
WIDTH = 8192
KVW = 1024
BLK = 256
NQ = KVW // BLK
CHIPS = 16
X = 4
PART = ROWS // X
MESH = pl.DeviceIdType.MESH

NODES = (
    (0, 1), (0, -1), (1, 0), (-1, 0), (2, 0),
    (1, 1), (-1, 1), (1, -1), (-1, -1), (0, 2),
    (2, 1), (2, -1), (1, 2), (-1, 2), (2, 2),
)
PARENTS = {
    (0, 1): (0, 0), (0, -1): (0, 0), (1, 0): (0, 0), (-1, 0): (0, 0), (2, 0): (1, 0),
    (1, 1): (0, 1), (-1, 1): (0, 1), (1, -1): (0, -1), (-1, -1): (0, -1), (0, 2): (0, 1),
    (2, 1): (-1, 1), (2, -1): (1, -1), (1, 2): (1, 1), (-1, 2): (-1, -1), (2, 2): (-1, 2),
}
TREES = (PARENTS, PARENTS | {(-1, 2): (0, 2)}, PARENTS, PARENTS | {(1, 2): (0, 2)})
ORDER = (
    -2, -3, -49, -33, -47, -16, -4, -17, 1, -1, -18, 46, 8, -34, 16,
    15, -32, 17, 0, 21, -46, 33, 13, 100, 32, 52, 25, 24, 19, 7,
    9, 22, -19, 53, -31, 3, 20, 31, 28, 58, 11, -48, 2, 18, 101,
    5, 26, 23, 45, 56, 6, 29, 30, 48, 27, 47, 34, 14, 59, 12,
    38, 51, 54, 37, 36, 10, 35, 4, 39, 102, 43, 50, 55, 40, 57,
    49, 42, 41, 44,
)
GROUP = 4
RECEIVES = [code for code in ORDER if 0 <= code < 100]
OUTER = 100
LATE = RECEIVES[-1] // 15 - 2


def kernel(
    tokens, queries, segs, weights, params, moment,
    mixed, late_probs, late_values, gv, mv,
    gathered, feats, acc, incoming, qv, bias, probs, keys,
    raw, partsum, partin, total,
    gsend, grecv, tsend, trecv, xsend, xrecv, zsend, zrecv, bsend, brecv, psend, precv,
    own_sem, feat_sem, q_sem, raw_sem, g_sem, m_sem,
):
    r = lax.axis_index("replica")
    f = lax.axis_index("fsdp")
    zl, x = r // X, r % X
    y, zh, c = f // 8, (f // 2) % 4, f % 2
    sign = 1 - 2 * c
    other = 1 - c
    sibling = (r, f + 1 - 2 * c)
    zpeer = ((1 - zl) * X + x, f)

    def xpeer(step):
        return (zl * X + (x + step) % X, f)

    def dev(dy, dz):
        return (r, (((y + dy + 4) % 4) * 4 + (zh + dz * sign + 4) % 4) * 2 + c)

    def slot(node):
        return ((y - node[0] + 4) % 4) * 4 + (zh - node[1] * sign + 4) % 4

    own = y * 4 + zh

    own_feats = [
        pltpu.make_async_copy(
            tokens.at[:, pl.ds(pl.multiple_of((2 * o + c) * BLK, BLK), BLK)],
            feats.at[o, pl.ds(pl.multiple_of(c * ROWS, ROWS), ROWS)],
            feat_sem,
        )
        for o in range(CHIPS)
    ]
    own_weights = [
        pltpu.make_async_copy(weights.at[:, pl.ds(q * BLK, BLK)], gathered.at[own, q], own_sem.at[q])
        for q in range(NQ)
    ]
    q_copy = pltpu.make_async_copy(queries, qv, q_sem)
    g_copy = pltpu.make_async_copy(params, gv, g_sem)
    m_copy = pltpu.make_async_copy(moment, mv, m_sem)
    raw_copy = pltpu.make_async_copy(weights.at[pl.ds(pl.multiple_of(x * PART, PART), PART)], raw.at[x], raw_sem)

    barrier = pltpu.get_barrier_semaphore()
    peers = [dev(1, 0), dev(-1, 0), dev(0, 1), dev(0, -1), sibling, zpeer, xpeer(1), xpeer(2), xpeer(3)]
    for peer in peers:
        pl.semaphore_signal(barrier, inc=1, device_id=peer, device_id_type=MESH)
    for copy in own_weights + own_feats:
        copy.start()
    raw_copy.start()
    pl.semaphore_wait(barrier, len(peers))

    def hop(q, child):
        node = TREES[q][child]
        at, index = slot(node), NODES.index(child)
        source = weights.at[:, pl.ds(q * BLK, BLK)] if node == (0, 0) else gathered.at[at, q]
        return pltpu.make_async_remote_copy(
            src_ref=source, dst_ref=gathered.at[at, q],
            send_sem=gsend.at[q, index], recv_sem=grecv.at[q, index],
            device_id=dev(*step_of(q, child)), device_id_type=MESH,
        )

    def step_of(q, child):
        node = TREES[q][child]
        dy, dz = (child[0] - node[0]) % 4, (child[1] - node[1]) % 4
        return (dy - 4 if dy == 3 else dy, dz - 4 if dz == 3 else dz)

    def arrive(q, node):
        at, index = slot(node), NODES.index(node)
        pltpu.make_async_remote_copy(
            src_ref=gathered.at[at, q], dst_ref=gathered.at[at, q],
            send_sem=gsend.at[q, index], recv_sem=grecv.at[q, index],
            device_id=sibling, device_id_type=MESH,
        ).wait_recv()

    def feat_send(o):
        return pltpu.make_async_remote_copy(
            src_ref=tokens.at[:, pl.ds(pl.multiple_of((2 * o + other) * BLK, BLK), BLK)],
            dst_ref=feats.at[o, pl.ds(pl.multiple_of(c * ROWS, ROWS), ROWS)],
            send_sem=tsend, recv_sem=trecv, device_id=sibling, device_id_type=MESH,
        )

    def all_feats(row_core):
        view = feats.at[:, pl.ds(pl.multiple_of(row_core * ROWS, ROWS), ROWS)]
        return pltpu.make_async_remote_copy(
            src_ref=view, dst_ref=view, send_sem=tsend, recv_sem=trecv, device_id=sibling, device_id_type=MESH
        )

    def raw_send(step):
        to = (x + step) % X
        return pltpu.make_async_remote_copy(
            src_ref=weights.at[pl.ds(pl.multiple_of(to * PART, PART), PART)], dst_ref=raw.at[x],
            send_sem=xsend.at[step - 1], recv_sem=xrecv.at[step - 1], device_id=xpeer(step), device_id_type=MESH,
        )

    def raw_arrive(step):
        at = (x - step + X) % X
        pltpu.make_async_remote_copy(
            src_ref=raw.at[at], dst_ref=raw.at[at],
            send_sem=xsend.at[step - 1], recv_sem=xrecv.at[step - 1], device_id=xpeer(step), device_id_type=MESH,
        ).wait_recv()

    z_copy = pltpu.make_async_remote_copy(
        src_ref=partsum, dst_ref=partin, send_sem=zsend, recv_sem=zrecv, device_id=zpeer, device_id_type=MESH
    )

    def spread(step):
        return pltpu.make_async_remote_copy(
            src_ref=total.at[x], dst_ref=total.at[x],
            send_sem=bsend.at[step - 1], recv_sem=brecv.at[step - 1], device_id=xpeer(step), device_id_type=MESH,
        )

    def spread_arrive(step):
        at = (x - step + X) % X
        pltpu.make_async_remote_copy(
            src_ref=total.at[at], dst_ref=total.at[at],
            send_sem=bsend.at[step - 1], recv_sem=brecv.at[step - 1], device_id=xpeer(step), device_id_type=MESH,
        ).wait_recv()

    def exchange(q):
        return pltpu.make_async_remote_copy(
            src_ref=acc.at[q, pl.ds(pl.multiple_of(other * ROWS, ROWS), ROWS)], dst_ref=incoming.at[q],
            send_sem=psend.at[q], recv_sem=precv.at[q], device_id=sibling, device_id_type=MESH,
        )

    def multiply(q, nodes, fresh=False):
        slots = [slot(node) for node in nodes]

        @pl.loop(0, 2)
        def _(half):
            at = pl.ds(pl.multiple_of(half * ROWS, ROWS), ROWS)
            partial = None
            for s in slots:
                term = jnp.dot(feats[s, at, :], gathered[s, q], preferred_element_type=jnp.float32)
                partial = term if partial is None else partial + term
            acc[q, at, :] = partial if fresh else acc[q, at, :] + partial

    def finish_block(q):
        mine = acc[q, pl.ds(pl.multiple_of(c * ROWS, ROWS), ROWS), :]
        return ((mine + incoming[q]) * WIDTH ** (-0.5)).astype(jnp.bfloat16)

    def softmax_heads(start):
        kv = start // Q_GROUP

        @pl.loop(0, 2)
        def _(i):
            h = start + i
            head = qv[:, pl.ds(pl.multiple_of(h * HD, HD), HD)]
            scores = lax.dot_general(
                head, keys[:, kv * HD : (kv + 1) * HD], (((1,), (1,)), ((), ())), preferred_element_type=jnp.float32
            )
            scores = scores * (HD ** (-0.5) * math.log2(math.e)) + bias[...]
            top = jnp.max(scores, axis=1, keepdims=True)
            weight = jnp.exp2(scores - top)
            norm = 1.0 / jnp.sum(weight, axis=1, keepdims=True)
            target = late_probs if start // (2 * Q_GROUP) == LATE else probs
            target[lax.rem(h, 2 * Q_GROUP)] = (weight * norm).astype(jnp.bfloat16)

    def mix(q):
        block = finish_block(q)
        for j in range(2):
            values = block[:, j * HD : (j + 1) * HD]

            @pl.loop(0, Q_GROUP)
            def _(i):
                h = j * Q_GROUP + i
                out = jnp.dot(probs[h], values, preferred_element_type=jnp.float32)
                mixed[:, pl.ds(pl.multiple_of(h * HD, HD), HD)] = out.astype(jnp.bfloat16)

    def sum_raw():
        for step in (1, 2, 3):
            raw_arrive(step)
        raw_copy.wait()
        partsum[...] = (
            raw[0].astype(jnp.float32) + raw[1].astype(jnp.float32) + raw[2].astype(jnp.float32) + raw[3].astype(jnp.float32)
        )
        z_copy.start()

    def spread_total():
        z_copy.wait()
        total[x] = partsum[...] + partin[...]
        for step in (1, 2, 3):
            spread(step).start()

    def update():
        for step in (1, 2, 3):
            spread_arrive(step)
        g_copy.wait()
        m_copy.wait()

        @pl.loop(0, X)
        def _(j):
            at = pl.ds(pl.multiple_of(j * PART, PART), PART)
            g = gv[at, :]
            grad = g - total[j] * 0.125
            fresh = 0.9 * mv[at, :] + grad
            mv[at, :] = fresh
            gv[at, :] = g - 0.7 * (grad + 0.9 * fresh)

    pending = {q: [] for q in range(NQ)}
    left = {q: CHIPS - 1 for q in range(NQ)}
    started = set()
    todo = []
    state = {"ready": False, "queries": False}

    def flush(q):
        if pending[q]:
            multiply(q, pending[q], fresh=q not in started)
            started.add(q)
            pending[q] = []

    def settle(q):
        exchange(q).wait_recv()
        if q < 2:
            keys[:, q * BLK : (q + 1) * BLK] = finish_block(q)
            if not state["queries"]:
                state["queries"] = True
                q_copy.wait()
            todo.extend(range(q * 2 * Q_GROUP, (q + 1) * 2 * Q_GROUP, 2))
        elif q - 2 == LATE:
            late_values[...] = finish_block(q)
        else:
            mix(q)

    waiting = []
    done = 0
    opened = False
    for code in ORDER:
        if code < 0:
            q, n = divmod(-code - 1, 15)
            hop(q, NODES[n]).start()
            continue
        if code >= OUTER:
            (sum_raw, spread_total, update)[code - OUTER]()
            continue
        if not opened:
            opened = True
            for step in (1, 2, 3):
                raw_send(step).start()
            for o in range(CHIPS):
                feat_send(o).start()
            q_copy.start()
            g_copy.start()
            m_copy.start()
            row = lax.broadcast_in_dim(segs[...], (ROWS, ROWS), (0, 1))
            t_at = lax.broadcasted_iota(jnp.int32, (ROWS, ROWS), 0)
            s_at = lax.broadcasted_iota(jnp.int32, (ROWS, ROWS), 1)
            allowed = (row == row.T) & (s_at <= t_at)
            bias[...] = jnp.where(allowed, 0.0, -1e30)
        q, n = divmod(code, 15)
        arrive(q, NODES[n])
        for child in NODES:
            if TREES[q][child] == NODES[n]:
                hop(q, child).start()
        done += 1
        pending[q].append(NODES[n])
        left[q] -= 1
        if not state["ready"] and done >= 4:
            state["ready"] = True
            for o in own_weights:
                o.wait()
            view = feats.at[:, pl.ds(pl.multiple_of(c * ROWS, ROWS), ROWS)]
            pltpu.make_async_copy(view, view, feat_sem).wait()
            all_feats(other).wait_recv()
            for qq in range(NQ):
                pending[qq].append((0, 0))
        if state["ready"] and (len(pending[q]) >= GROUP or left[q] == 0):
            flush(q)
        for item in list(waiting):
            if done >= item[0] + 2 and (item[1] < 2 or not todo):
                waiting.remove(item)
                settle(item[1])
        if left[q] == 0:
            exchange(q).start()
            waiting.append((done, q))
        remaining = len(RECEIVES) - done
        if todo:
            count = -(-len(todo) // max(1, remaining - 3))
            for start in todo[:count]:
                softmax_heads(start)
            del todo[:count]

    for start in todo:
        softmax_heads(start)
    for _, q in waiting:
        settle(q)

    for q in range(NQ):
        for child in NODES:
            hop(q, child).wait_send()
        exchange(q).wait_send()
    all_feats(other).wait_send()
    for step in (1, 2, 3):
        raw_send(step).wait_send()
        spread(step).wait_send()


def finish_kernel(
    mixed, late_probs, late_values, gv, mv, attended, new_params, new_moment, late_mixed, early_sem, late_sem, p_sem, m_sem
):
    half = 2 * Q_GROUP * HD
    piece = Q_GROUP * HD
    early = pltpu.make_async_copy(mixed, attended.at[:, pl.ds((1 - LATE) * half, half)], early_sem)
    copies = [early, pltpu.make_async_copy(gv, new_params, p_sem), pltpu.make_async_copy(mv, new_moment, m_sem)]
    for copy in copies:
        copy.start()
    for j in range(2):
        values = late_values[:, j * HD : (j + 1) * HD]
        for i in range(Q_GROUP):
            h = j * Q_GROUP + i
            out = jnp.dot(late_probs[h], values, preferred_element_type=jnp.float32)
            late_mixed[:, h * HD : (h + 1) * HD] = out.astype(jnp.bfloat16)
        copy = pltpu.make_async_copy(
            late_mixed.at[:, pl.ds(j * piece, piece)],
            attended.at[:, pl.ds(LATE * half + j * piece, piece)],
            late_sem.at[j],
        )
        copy.start()
        copies.append(copy)
    for copy in copies:
        copy.wait()


def shards(tokens, queries, segments, local_weights, global_params, momentum):
    hbm = pl.BlockSpec(memory_space=pltpu.HBM)
    any_space = pl.BlockSpec(memory_space=pl.ANY)
    vmem = pl.BlockSpec(memory_space=pltpu.VMEM)
    dma = pltpu.SemaphoreType.DMA
    half = 2 * Q_GROUP
    kept = pl.pallas_call(
        kernel,
        out_shape=(
            pltpu.VMEM((ROWS, half * HD), jnp.bfloat16),
            pltpu.VMEM((half, ROWS, ROWS), jnp.bfloat16),
            pltpu.VMEM((ROWS, BLK), jnp.bfloat16),
            pltpu.VMEM((ROWS, KVW), jnp.float32),
            pltpu.VMEM((ROWS, KVW), jnp.float32),
        ),
        in_specs=[hbm, hbm, vmem, hbm, hbm, hbm],
        out_specs=(vmem,) * 5,
        scratch_shapes=[
            pltpu.VMEM((CHIPS, NQ, BLK, BLK), jnp.bfloat16),
            pltpu.VMEM((CHIPS, 2 * ROWS, BLK), jnp.bfloat16),
            pltpu.VMEM((NQ, 2 * ROWS, BLK), jnp.float32),
            pltpu.VMEM((NQ, ROWS, BLK), jnp.float32),
            pltpu.VMEM((ROWS, QH * HD), jnp.bfloat16),
            pltpu.VMEM((ROWS, ROWS), jnp.float32),
            pltpu.VMEM((half, ROWS, ROWS), jnp.bfloat16),
            pltpu.VMEM((ROWS, 2 * BLK), jnp.bfloat16),
            pltpu.VMEM((X, PART, KVW), jnp.bfloat16),
            pltpu.VMEM((PART, KVW), jnp.float32),
            pltpu.VMEM((PART, KVW), jnp.float32),
            pltpu.VMEM((X, PART, KVW), jnp.float32),
            dma((NQ, 15)), dma((NQ, 15)), dma, dma, dma((3,)), dma((3,)), dma, dma, dma((3,)), dma((3,)),
            dma((NQ,)), dma((NQ,)),
            dma((NQ,)), dma, dma, dma, dma, dma,
        ],
        compiler_params=pltpu.CompilerParams(
            collective_id=0, has_side_effects=True, vmem_limit_bytes=57 * 2**20
        ),
        cost_estimate=pl.CostEstimate(flops=6 * 10**9, bytes_accessed=13 * 2**20, transcendentals=2**21),
        name="sync_and_attend",
    )(tokens[0], queries[0], segments[0], local_weights[0], global_params, momentum)
    attended, new_params, new_momentum = pl.pallas_call(
        finish_kernel,
        out_shape=(
            jax.ShapeDtypeStruct((ROWS, QH * HD), jnp.bfloat16),
            jax.ShapeDtypeStruct((ROWS, KVW), jnp.float32),
            jax.ShapeDtypeStruct((ROWS, KVW), jnp.float32),
        ),
        in_specs=[vmem] * 5,
        out_specs=(any_space,) * 3,
        scratch_shapes=[pltpu.VMEM((ROWS, half * HD), jnp.bfloat16), dma, dma((2,)), dma, dma],
        compiler_params=pltpu.CompilerParams(vmem_limit_bytes=16 * 2**20),
        name="finish",
    )(*kept)
    return (attended[None], new_params, new_momentum)


def solution(mesh):
    placed = (
        P("replica", "fsdp", None),
        P("replica", "fsdp", None),
        P("replica", "fsdp", None),
        P("replica", "fsdp", None),
        P("fsdp", None),
        P("fsdp", None),
    )
    return jax.shard_map(
        shards,
        mesh=mesh,
        in_specs=placed,
        out_specs=(P("replica", "fsdp", None), P("fsdp", None), P("fsdp", None)),
        check_vma=False,
    )
```

```python
import math

import jax
import jax.numpy as jnp
from jax import lax
from jax.experimental import pallas as pl
from jax.experimental.pallas import tpu as pltpu
from jax.sharding import PartitionSpec as P

HD = 128
QH = 32
Q_GROUP = 8
ROWS = 256
WIDTH = 8192
KVW = 1024
BLK = 256
NQ = KVW // BLK
CHIPS = 16
X = 4
PART = ROWS // X
MESH = pl.DeviceIdType.MESH

NODES = (
    (0, 1), (0, -1), (1, 0), (-1, 0), (2, 0),
    (1, 1), (-1, 1), (1, -1), (-1, -1), (0, 2),
    (2, 1), (2, -1), (1, 2), (-1, 2), (2, 2),
)
PARENTS = {
    (0, 1): (0, 0), (0, -1): (0, 0), (1, 0): (0, 0), (-1, 0): (0, 0), (2, 0): (1, 0),
    (1, 1): (0, 1), (-1, 1): (0, 1), (1, -1): (0, -1), (-1, -1): (0, -1), (0, 2): (0, 1),
    (2, 1): (-1, 1), (2, -1): (1, -1), (1, 2): (1, 1), (-1, 2): (-1, -1), (2, 2): (-1, 2),
}
TREES = (PARENTS, PARENTS | {(-1, 2): (0, 2)}, PARENTS, PARENTS | {(1, 2): (0, 2)})
ORDER = (
    -2, -3, -49, -33, -47, -16, -4, -17, 1, -1, -18, 46, 8, -34, 16,
    15, -32, 17, 0, 21, -46, 33, 13, 100, 32, 52, 25, 24, 19, 7,
    9, 22, -19, 53, -31, 3, 20, 31, 28, 58, 11, -48, 2, 18, 101,
    5, 26, 23, 45, 56, 6, 29, 30, 48, 27, 47, 34, 14, 59, 12,
    38, 51, 54, 37, 36, 10, 35, 4, 39, 102, 43, 50, 55, 40, 57,
    49, 42, 41, 44,
)
GROUP = 4
RECEIVES = [code for code in ORDER if 0 <= code < 100]
OUTER = 100
TAIL = 55
LATE = RECEIVES[-1] // 15 - 2


def kernel(
    tokens, queries, segs, weights, params, moment,
    mixed, late_probs, late_values, gv, mv,
    gathered, feats, acc, incoming, qv, bias, probs, keys,
    raw, partsum, partin, total,
    gsend, grecv, tsend, trecv, xsend, xrecv, zsend, zrecv, bsend, brecv, psend, precv,
    own_sem, feat_sem, q_sem, raw_sem, g_sem, m_sem,
):
    r = lax.axis_index("replica")
    f = lax.axis_index("fsdp")
    zl, x = r // X, r % X
    y, zh, c = f // 8, (f // 2) % 4, f % 2
    sign = 1 - 2 * c
    other = 1 - c
    sibling = (r, f + 1 - 2 * c)
    zpeer = ((1 - zl) * X + x, f)

    def xpeer(step):
        return (zl * X + (x + step) % X, f)

    def dev(dy, dz):
        return (r, (((y + dy + 4) % 4) * 4 + (zh + dz * sign + 4) % 4) * 2 + c)

    def slot(node):
        return ((y - node[0] + 4) % 4) * 4 + (zh - node[1] * sign + 4) % 4

    own = y * 4 + zh

    own_feats = [
        pltpu.make_async_copy(
            tokens.at[:, pl.ds(pl.multiple_of((2 * o + c) * BLK, BLK), BLK)],
            feats.at[o, pl.ds(pl.multiple_of(c * ROWS, ROWS), ROWS)],
            feat_sem,
        )
        for o in range(CHIPS)
    ]
    own_weights = [
        pltpu.make_async_copy(weights.at[:, pl.ds(q * BLK, BLK)], gathered.at[own, q], own_sem.at[q])
        for q in range(NQ)
    ]
    q_copy = pltpu.make_async_copy(queries, qv, q_sem)
    g_copy = pltpu.make_async_copy(params, gv, g_sem)
    m_copy = pltpu.make_async_copy(moment, mv, m_sem)
    raw_copy = pltpu.make_async_copy(weights.at[pl.ds(pl.multiple_of(x * PART, PART), PART)], raw.at[x], raw_sem)

    barrier = pltpu.get_barrier_semaphore()
    peers = [dev(1, 0), dev(-1, 0), dev(0, 1), dev(0, -1), sibling, zpeer, xpeer(1), xpeer(2), xpeer(3)]
    for peer in peers:
        pl.semaphore_signal(barrier, inc=1, device_id=peer, device_id_type=MESH)
    for copy in own_weights + own_feats:
        copy.start()
    raw_copy.start()
    pl.semaphore_wait(barrier, len(peers))

    def hop(q, child):
        node = TREES[q][child]
        at, index = slot(node), NODES.index(child)
        source = weights.at[:, pl.ds(q * BLK, BLK)] if node == (0, 0) else gathered.at[at, q]
        return pltpu.make_async_remote_copy(
            src_ref=source, dst_ref=gathered.at[at, q],
            send_sem=gsend.at[q, index], recv_sem=grecv.at[q, index],
            device_id=dev(*step_of(q, child)), device_id_type=MESH,
        )

    def step_of(q, child):
        node = TREES[q][child]
        dy, dz = (child[0] - node[0]) % 4, (child[1] - node[1]) % 4
        return (dy - 4 if dy == 3 else dy, dz - 4 if dz == 3 else dz)

    def arrive(q, node):
        at, index = slot(node), NODES.index(node)
        pltpu.make_async_remote_copy(
            src_ref=gathered.at[at, q], dst_ref=gathered.at[at, q],
            send_sem=gsend.at[q, index], recv_sem=grecv.at[q, index],
            device_id=sibling, device_id_type=MESH,
        ).wait_recv()

    def feat_send(o):
        return pltpu.make_async_remote_copy(
            src_ref=tokens.at[:, pl.ds(pl.multiple_of((2 * o + other) * BLK, BLK), BLK)],
            dst_ref=feats.at[o, pl.ds(pl.multiple_of(c * ROWS, ROWS), ROWS)],
            send_sem=tsend, recv_sem=trecv, device_id=sibling, device_id_type=MESH,
        )

    def all_feats(row_core):
        view = feats.at[:, pl.ds(pl.multiple_of(row_core * ROWS, ROWS), ROWS)]
        return pltpu.make_async_remote_copy(
            src_ref=view, dst_ref=view, send_sem=tsend, recv_sem=trecv, device_id=sibling, device_id_type=MESH
        )

    def raw_send(step):
        to = (x + step) % X
        return pltpu.make_async_remote_copy(
            src_ref=weights.at[pl.ds(pl.multiple_of(to * PART, PART), PART)], dst_ref=raw.at[x],
            send_sem=xsend.at[step - 1], recv_sem=xrecv.at[step - 1], device_id=xpeer(step), device_id_type=MESH,
        )

    def raw_arrive(step):
        at = (x - step + X) % X
        pltpu.make_async_remote_copy(
            src_ref=raw.at[at], dst_ref=raw.at[at],
            send_sem=xsend.at[step - 1], recv_sem=xrecv.at[step - 1], device_id=xpeer(step), device_id_type=MESH,
        ).wait_recv()

    z_copy = pltpu.make_async_remote_copy(
        src_ref=partsum, dst_ref=partin, send_sem=zsend, recv_sem=zrecv, device_id=zpeer, device_id_type=MESH
    )

    def spread(step):
        return pltpu.make_async_remote_copy(
            src_ref=total.at[x], dst_ref=total.at[x],
            send_sem=bsend.at[step - 1], recv_sem=brecv.at[step - 1], device_id=xpeer(step), device_id_type=MESH,
        )

    def spread_arrive(step):
        at = (x - step + X) % X
        pltpu.make_async_remote_copy(
            src_ref=total.at[at], dst_ref=total.at[at],
            send_sem=bsend.at[step - 1], recv_sem=brecv.at[step - 1], device_id=xpeer(step), device_id_type=MESH,
        ).wait_recv()

    def exchange(q):
        return pltpu.make_async_remote_copy(
            src_ref=acc.at[q, pl.ds(pl.multiple_of(other * ROWS, ROWS), ROWS)], dst_ref=incoming.at[q],
            send_sem=psend.at[q], recv_sem=precv.at[q], device_id=sibling, device_id_type=MESH,
        )

    def multiply(q, nodes, fresh=False):
        partial = None
        for s in [slot(node) for node in nodes]:
            term = jnp.dot(feats[s], gathered[s, q], preferred_element_type=jnp.float32)
            partial = term if partial is None else partial + term
        acc[q] = partial if fresh else acc[q] + partial

    def finish_block(q):
        mine = acc[q, pl.ds(pl.multiple_of(c * ROWS, ROWS), ROWS), :]
        return ((mine + incoming[q]) * WIDTH ** (-0.5)).astype(jnp.bfloat16)

    def softmax_heads(start):
        kv = start // Q_GROUP
        target = late_probs if start // (2 * Q_GROUP) == LATE else probs
        for h in range(start, start + 2):
            scores = lax.dot_general(
                qv[:, h * HD : (h + 1) * HD], keys[:, kv * HD : (kv + 1) * HD],
                (((1,), (1,)), ((), ())), preferred_element_type=jnp.float32,
            )
            scores = scores * (HD ** (-0.5) * math.log2(math.e)) + bias[...]
            top = jnp.max(scores, axis=1, keepdims=True)
            weight = jnp.exp2(scores - top)
            norm = 1.0 / jnp.sum(weight, axis=1, keepdims=True)
            target[h % (2 * Q_GROUP)] = (weight * norm).astype(jnp.bfloat16)

    def mix(q):
        block = finish_block(q)
        for j in range(2):
            values = block[:, j * HD : (j + 1) * HD]

            for h in range(j * Q_GROUP, (j + 1) * Q_GROUP):
                out = jnp.dot(probs[h], values, preferred_element_type=jnp.float32)
                mixed[:, h * HD : (h + 1) * HD] = out.astype(jnp.bfloat16)

    def sum_raw():
        for step in (1, 2, 3):
            raw_arrive(step)
        raw_copy.wait()
        partsum[...] = (
            raw[0].astype(jnp.float32) + raw[1].astype(jnp.float32) + raw[2].astype(jnp.float32) + raw[3].astype(jnp.float32)
        )
        z_copy.start()

    def spread_total():
        z_copy.wait()
        total[x] = partsum[...] + partin[...]
        for step in (1, 2, 3):
            spread(step).start()

    def update():
        for step in (1, 2, 3):
            spread_arrive(step)
        g_copy.wait()
        m_copy.wait()

        @pl.loop(0, X)
        def _(j):
            at = pl.ds(pl.multiple_of(j * PART, PART), PART)
            g = gv[at, :]
            grad = g - total[j] * 0.125
            fresh = 0.9 * mv[at, :] + grad
            mv[at, :] = fresh
            gv[at, :] = g - 0.7 * (grad + 0.9 * fresh)

    pending = {q: [] for q in range(NQ)}
    left = {q: CHIPS - 1 for q in range(NQ)}
    started = set()
    todo = []
    state = {"ready": False, "queries": False}

    def flush(q):
        if pending[q]:
            multiply(q, pending[q], fresh=q not in started)
            started.add(q)
            pending[q] = []

    def settle(q):
        exchange(q).wait_recv()
        if q < 2:
            keys[:, q * BLK : (q + 1) * BLK] = finish_block(q)
            if not state["queries"]:
                state["queries"] = True
                q_copy.wait()
            todo.extend(range(q * 2 * Q_GROUP, (q + 1) * 2 * Q_GROUP, 2))
        elif q - 2 == LATE:
            late_values[...] = finish_block(q)
        else:
            mix(q)

    waiting = []
    done = 0
    opened = False
    for code in ORDER:
        if code < 0:
            q, n = divmod(-code - 1, 15)
            hop(q, NODES[n]).start()
            continue
        if code >= OUTER:
            (sum_raw, spread_total, update)[code - OUTER]()
            continue
        if not opened:
            opened = True
            for step in (1, 2, 3):
                raw_send(step).start()
            for o in range(CHIPS):
                feat_send(o).start()
            q_copy.start()
            g_copy.start()
            m_copy.start()
            row = lax.broadcast_in_dim(segs[...], (ROWS, ROWS), (0, 1))
            t_at = lax.broadcasted_iota(jnp.int32, (ROWS, ROWS), 0)
            s_at = lax.broadcasted_iota(jnp.int32, (ROWS, ROWS), 1)
            allowed = (row == row.T) & (s_at <= t_at)
            bias[...] = jnp.where(allowed, 0.0, -1e30)
        q, n = divmod(code, 15)
        arrive(q, NODES[n])
        for child in NODES:
            if TREES[q][child] == NODES[n]:
                hop(q, child).start()
        done += 1
        pending[q].append(NODES[n])
        left[q] -= 1
        if not state["ready"] and done >= 4:
            state["ready"] = True
            for o in own_weights:
                o.wait()
            view = feats.at[:, pl.ds(pl.multiple_of(c * ROWS, ROWS), ROWS)]
            pltpu.make_async_copy(view, view, feat_sem).wait()
            all_feats(other).wait_recv()
            for qq in range(NQ):
                pending[qq].append((0, 0))
        if state["ready"] and (len(pending[q]) >= GROUP or left[q] == 0 or done > TAIL):
            flush(q)
        for item in list(waiting):
            if done >= item[0] + 2 and (item[1] < 2 or not todo):
                waiting.remove(item)
                settle(item[1])
        if left[q] == 0:
            exchange(q).start()
            waiting.append((done, q))
        remaining = len(RECEIVES) - done
        if todo:
            count = -(-len(todo) // max(1, remaining - 3))
            for start in todo[:count]:
                softmax_heads(start)
            del todo[:count]

    for start in todo:
        softmax_heads(start)
    for _, q in waiting:
        settle(q)

    for q in range(NQ):
        for child in NODES:
            hop(q, child).wait_send()
        exchange(q).wait_send()
    all_feats(other).wait_send()
    for step in (1, 2, 3):
        raw_send(step).wait_send()
        spread(step).wait_send()


def finish_kernel(
    mixed, late_probs, late_values, gv, mv, attended, new_params, new_moment, late_mixed, early_sem, late_sem, p_sem, m_sem
):
    half = 2 * Q_GROUP * HD
    piece = Q_GROUP * HD
    early = pltpu.make_async_copy(mixed, attended.at[:, pl.ds((1 - LATE) * half, half)], early_sem)
    copies = [early, pltpu.make_async_copy(gv, new_params, p_sem), pltpu.make_async_copy(mv, new_moment, m_sem)]
    for copy in copies:
        copy.start()
    for j in range(2):
        values = late_values[:, j * HD : (j + 1) * HD]
        for i in range(Q_GROUP):
            h = j * Q_GROUP + i
            out = jnp.dot(late_probs[h], values, preferred_element_type=jnp.float32)
            late_mixed[:, h * HD : (h + 1) * HD] = out.astype(jnp.bfloat16)
        copy = pltpu.make_async_copy(
            late_mixed.at[:, pl.ds(j * piece, piece)],
            attended.at[:, pl.ds(LATE * half + j * piece, piece)],
            late_sem.at[j],
        )
        copy.start()
        copies.append(copy)
    for copy in copies:
        copy.wait()


def shards(tokens, queries, segments, local_weights, global_params, momentum):
    hbm = pl.BlockSpec(memory_space=pltpu.HBM)
    any_space = pl.BlockSpec(memory_space=pl.ANY)
    vmem = pl.BlockSpec(memory_space=pltpu.VMEM)
    dma = pltpu.SemaphoreType.DMA
    half = 2 * Q_GROUP
    kept = pl.pallas_call(
        kernel,
        out_shape=(
            pltpu.VMEM((ROWS, half * HD), jnp.bfloat16),
            pltpu.VMEM((half, ROWS, ROWS), jnp.bfloat16),
            pltpu.VMEM((ROWS, BLK), jnp.bfloat16),
            pltpu.VMEM((ROWS, KVW), jnp.float32),
            pltpu.VMEM((ROWS, KVW), jnp.float32),
        ),
        in_specs=[hbm, hbm, vmem, hbm, hbm, hbm],
        out_specs=(vmem,) * 5,
        scratch_shapes=[
            pltpu.VMEM((CHIPS, NQ, BLK, BLK), jnp.bfloat16),
            pltpu.VMEM((CHIPS, 2 * ROWS, BLK), jnp.bfloat16),
            pltpu.VMEM((NQ, 2 * ROWS, BLK), jnp.float32),
            pltpu.VMEM((NQ, ROWS, BLK), jnp.float32),
            pltpu.VMEM((ROWS, QH * HD), jnp.bfloat16),
            pltpu.VMEM((ROWS, ROWS), jnp.float32),
            pltpu.VMEM((half, ROWS, ROWS), jnp.bfloat16),
            pltpu.VMEM((ROWS, 2 * BLK), jnp.bfloat16),
            pltpu.VMEM((X, PART, KVW), jnp.bfloat16),
            pltpu.VMEM((PART, KVW), jnp.float32),
            pltpu.VMEM((PART, KVW), jnp.float32),
            pltpu.VMEM((X, PART, KVW), jnp.float32),
            dma((NQ, 15)), dma((NQ, 15)), dma, dma, dma((3,)), dma((3,)), dma, dma, dma((3,)), dma((3,)),
            dma((NQ,)), dma((NQ,)),
            dma((NQ,)), dma, dma, dma, dma, dma,
        ],
        compiler_params=pltpu.CompilerParams(
            collective_id=0, has_side_effects=True, vmem_limit_bytes=57 * 2**20
        ),
        cost_estimate=pl.CostEstimate(flops=6 * 10**9, bytes_accessed=13 * 2**20, transcendentals=2**21),
        name="sync_and_attend",
    )(tokens[0], queries[0], segments[0], local_weights[0], global_params, momentum)
    attended, new_params, new_momentum = pl.pallas_call(
        finish_kernel,
        out_shape=(
            jax.ShapeDtypeStruct((ROWS, QH * HD), jnp.bfloat16),
            jax.ShapeDtypeStruct((ROWS, KVW), jnp.float32),
            jax.ShapeDtypeStruct((ROWS, KVW), jnp.float32),
        ),
        in_specs=[vmem] * 5,
        out_specs=(any_space,) * 3,
        scratch_shapes=[pltpu.VMEM((ROWS, half * HD), jnp.bfloat16), dma, dma((2,)), dma, dma],
        compiler_params=pltpu.CompilerParams(vmem_limit_bytes=16 * 2**20),
        name="finish",
    )(*kept)
    return (attended[None], new_params, new_momentum)


def solution(mesh):
    placed = (
        P("replica", "fsdp", None),
        P("replica", "fsdp", None),
        P("replica", "fsdp", None),
        P("replica", "fsdp", None),
        P("fsdp", None),
        P("fsdp", None),
    )
    return jax.shard_map(
        shards,
        mesh=mesh,
        in_specs=placed,
        out_specs=(P("replica", "fsdp", None), P("fsdp", None), P("fsdp", None)),
        check_vma=False,
    )
```

```python
import math

import jax
import jax.numpy as jnp
from jax import lax
from jax.experimental import pallas as pl
from jax.experimental.pallas import tpu as pltpu
from jax.sharding import PartitionSpec as P

HD = 128
QH = 32
Q_GROUP = 8
ROWS = 256
WIDTH = 8192
KVW = 1024
BLK = 256
NQ = KVW // BLK
CHIPS = 16
X = 4
PART = ROWS // X
MESH = pl.DeviceIdType.MESH

NODES = (
    (0, 1), (0, -1), (1, 0), (-1, 0), (2, 0),
    (1, 1), (-1, 1), (1, -1), (-1, -1), (0, 2),
    (2, 1), (2, -1), (1, 2), (-1, 2), (2, 2),
)
PARENTS = {
    (0, 1): (0, 0), (0, -1): (0, 0), (1, 0): (0, 0), (-1, 0): (0, 0), (2, 0): (1, 0),
    (1, 1): (0, 1), (-1, 1): (0, 1), (1, -1): (0, -1), (-1, -1): (0, -1), (0, 2): (0, 1),
    (2, 1): (-1, 1), (2, -1): (1, -1), (1, 2): (1, 1), (-1, 2): (-1, -1), (2, 2): (-1, 2),
}
TREES = (PARENTS | {(1, 2): (0, 2)}, PARENTS | {(-1, 2): (0, 2)}, PARENTS, PARENTS)
ORDER = (
    -33, -34, -2, -46, -18, -49, -16, -3, -47, -19, 1, -32, -4, 17, 15,
    -17, -1, 7, 45, 2, 46, 19, 31, 3, 8, -31, 100, 51, 24, 16,
    -48, 55, 0, 54, 28, 22, 20, 53, 37, 23, 21, 101, 13, 33, 6,
    48, 4, 5, 38, 30, 9, 27, 29, 47, 26, 52, 25, 18, 14, 58,
    50, 32, 11, 43, 35, 41, 12, 36, 10, 49, 39, 59, 56, 57, 42,
    44, 40, 34, 102,
)
GROUP = 4
RECEIVES = [code for code in ORDER if 0 <= code < 100]
OUTER = 100
TAIL = 55
LATE = RECEIVES[-1] // 15 - 2


def kernel(
    tokens, queries, segs, weights, params, moment,
    mixed, late_probs, late_values, gv, mv,
    gathered, feats, acc, incoming, qv, bias, probs, keys,
    raw, partsum, partin, total,
    gsend, grecv, tsend, trecv, xsend, xrecv, zsend, zrecv, bsend, brecv, psend, precv,
    own_sem, feat_sem, q_sem, raw_sem, g_sem, m_sem,
):
    r = lax.axis_index("replica")
    f = lax.axis_index("fsdp")
    zl, x = r // X, r % X
    y, zh, c = f // 8, (f // 2) % 4, f % 2
    sign = 1 - 2 * c
    other = 1 - c
    sibling = (r, f + 1 - 2 * c)
    zpeer = ((1 - zl) * X + x, f)

    def xpeer(step):
        return (zl * X + (x + step) % X, f)

    def dev(dy, dz):
        return (r, (((y + dy + 4) % 4) * 4 + (zh + dz * sign + 4) % 4) * 2 + c)

    def slot(node):
        return ((y - node[0] + 4) % 4) * 4 + (zh - node[1] * sign + 4) % 4

    own = y * 4 + zh

    own_feats = [
        pltpu.make_async_copy(
            tokens.at[:, pl.ds(pl.multiple_of((2 * o + c) * BLK, BLK), BLK)],
            feats.at[o, pl.ds(pl.multiple_of(c * ROWS, ROWS), ROWS)],
            feat_sem,
        )
        for o in range(CHIPS)
    ]
    own_weights = [
        pltpu.make_async_copy(weights.at[:, pl.ds(q * BLK, BLK)], gathered.at[own, q], own_sem.at[q])
        for q in range(NQ)
    ]
    q_copy = pltpu.make_async_copy(queries, qv, q_sem)
    g_copy = pltpu.make_async_copy(params, gv, g_sem)
    m_copy = pltpu.make_async_copy(moment, mv, m_sem)
    raw_copy = pltpu.make_async_copy(weights.at[pl.ds(pl.multiple_of(x * PART, PART), PART)], raw.at[x], raw_sem)

    barrier = pltpu.get_barrier_semaphore()
    peers = [dev(1, 0), dev(-1, 0), dev(0, 1), dev(0, -1), sibling, zpeer, xpeer(1), xpeer(2), xpeer(3)]
    for peer in peers:
        pl.semaphore_signal(barrier, inc=1, device_id=peer, device_id_type=MESH)
    for copy in own_weights + own_feats:
        copy.start()
    raw_copy.start()
    pl.semaphore_wait(barrier, len(peers))

    def hop(q, child):
        node = TREES[q][child]
        at, index = slot(node), NODES.index(child)
        source = weights.at[:, pl.ds(q * BLK, BLK)] if node == (0, 0) else gathered.at[at, q]
        return pltpu.make_async_remote_copy(
            src_ref=source, dst_ref=gathered.at[at, q],
            send_sem=gsend.at[q, index], recv_sem=grecv.at[q, index],
            device_id=dev(*step_of(q, child)), device_id_type=MESH,
        )

    def step_of(q, child):
        node = TREES[q][child]
        dy, dz = (child[0] - node[0]) % 4, (child[1] - node[1]) % 4
        return (dy - 4 if dy == 3 else dy, dz - 4 if dz == 3 else dz)

    def arrive(q, node):
        at, index = slot(node), NODES.index(node)
        pltpu.make_async_remote_copy(
            src_ref=gathered.at[at, q], dst_ref=gathered.at[at, q],
            send_sem=gsend.at[q, index], recv_sem=grecv.at[q, index],
            device_id=sibling, device_id_type=MESH,
        ).wait_recv()

    def feat_send(o):
        return pltpu.make_async_remote_copy(
            src_ref=tokens.at[:, pl.ds(pl.multiple_of((2 * o + other) * BLK, BLK), BLK)],
            dst_ref=feats.at[o, pl.ds(pl.multiple_of(c * ROWS, ROWS), ROWS)],
            send_sem=tsend, recv_sem=trecv, device_id=sibling, device_id_type=MESH,
        )

    def all_feats(row_core):
        view = feats.at[:, pl.ds(pl.multiple_of(row_core * ROWS, ROWS), ROWS)]
        return pltpu.make_async_remote_copy(
            src_ref=view, dst_ref=view, send_sem=tsend, recv_sem=trecv, device_id=sibling, device_id_type=MESH
        )

    def raw_send(step):
        to = (x + step) % X
        return pltpu.make_async_remote_copy(
            src_ref=weights.at[pl.ds(pl.multiple_of(to * PART, PART), PART)], dst_ref=raw.at[x],
            send_sem=xsend.at[step - 1], recv_sem=xrecv.at[step - 1], device_id=xpeer(step), device_id_type=MESH,
        )

    def raw_arrive(step):
        at = (x - step + X) % X
        pltpu.make_async_remote_copy(
            src_ref=raw.at[at], dst_ref=raw.at[at],
            send_sem=xsend.at[step - 1], recv_sem=xrecv.at[step - 1], device_id=xpeer(step), device_id_type=MESH,
        ).wait_recv()

    z_copy = pltpu.make_async_remote_copy(
        src_ref=partsum, dst_ref=partin, send_sem=zsend, recv_sem=zrecv, device_id=zpeer, device_id_type=MESH
    )

    def spread(step):
        return pltpu.make_async_remote_copy(
            src_ref=total.at[x], dst_ref=total.at[x],
            send_sem=bsend.at[step - 1], recv_sem=brecv.at[step - 1], device_id=xpeer(step), device_id_type=MESH,
        )

    def spread_arrive(step):
        at = (x - step + X) % X
        pltpu.make_async_remote_copy(
            src_ref=total.at[at], dst_ref=total.at[at],
            send_sem=bsend.at[step - 1], recv_sem=brecv.at[step - 1], device_id=xpeer(step), device_id_type=MESH,
        ).wait_recv()

    def exchange(q):
        return pltpu.make_async_remote_copy(
            src_ref=acc.at[q, pl.ds(pl.multiple_of(other * ROWS, ROWS), ROWS)], dst_ref=incoming.at[q],
            send_sem=psend.at[q], recv_sem=precv.at[q], device_id=sibling, device_id_type=MESH,
        )

    def multiply(q, nodes, fresh=False):
        partial = None
        for s in [slot(node) for node in nodes]:
            term = jnp.dot(feats[s], gathered[s, q], preferred_element_type=jnp.float32)
            partial = term if partial is None else partial + term
        acc[q] = partial if fresh else acc[q] + partial

    def finish_block(q):
        mine = acc[q, pl.ds(pl.multiple_of(c * ROWS, ROWS), ROWS), :]
        return ((mine + incoming[q]) * WIDTH ** (-0.5)).astype(jnp.bfloat16)

    def softmax_heads(start):
        kv = start // Q_GROUP
        target = late_probs if start // (2 * Q_GROUP) == LATE else probs
        for h in range(start, start + 2):
            scores = lax.dot_general(
                qv[:, h * HD : (h + 1) * HD], keys[:, kv * HD : (kv + 1) * HD],
                (((1,), (1,)), ((), ())), preferred_element_type=jnp.float32,
            )
            scores = scores * (HD ** (-0.5) * math.log2(math.e)) + bias[...]
            top = jnp.max(scores, axis=1, keepdims=True)
            weight = jnp.exp2(scores - top)
            norm = 1.0 / jnp.sum(weight, axis=1, keepdims=True)
            target[h % (2 * Q_GROUP)] = (weight * norm).astype(jnp.bfloat16)

    def mix(q):
        block = finish_block(q)
        for j in range(2):
            values = block[:, j * HD : (j + 1) * HD]

            for h in range(j * Q_GROUP, (j + 1) * Q_GROUP):
                out = jnp.dot(probs[h], values, preferred_element_type=jnp.float32)
                mixed[:, h * HD : (h + 1) * HD] = out.astype(jnp.bfloat16)

    def sum_raw():
        for step in (1, 2, 3):
            raw_arrive(step)
        raw_copy.wait()
        partsum[...] = (
            raw[0].astype(jnp.float32) + raw[1].astype(jnp.float32) + raw[2].astype(jnp.float32) + raw[3].astype(jnp.float32)
        )
        z_copy.start()

    def spread_total():
        z_copy.wait()
        total[x] = partsum[...] + partin[...]
        for step in (1, 2, 3):
            spread(step).start()

    def update():
        for step in (1, 2, 3):
            spread_arrive(step)
        g_copy.wait()
        m_copy.wait()

        @pl.loop(0, X)
        def _(j):
            at = pl.ds(pl.multiple_of(j * PART, PART), PART)
            g = gv[at, :]
            grad = g - total[j] * 0.125
            fresh = 0.9 * mv[at, :] + grad
            mv[at, :] = fresh
            gv[at, :] = g - 0.7 * (grad + 0.9 * fresh)

    pending = {q: [] for q in range(NQ)}
    left = {q: CHIPS - 1 for q in range(NQ)}
    started = set()
    todo = []
    state = {"ready": False, "queries": False}

    def flush(q):
        if pending[q]:
            multiply(q, pending[q], fresh=q not in started)
            started.add(q)
            pending[q] = []

    def settle(q):
        exchange(q).wait_recv()
        if q < 2:
            keys[:, q * BLK : (q + 1) * BLK] = finish_block(q)
            if not state["queries"]:
                state["queries"] = True
                q_copy.wait()
            todo.extend(range(q * 2 * Q_GROUP, (q + 1) * 2 * Q_GROUP, 2))
        elif q - 2 == LATE:
            late_values[...] = finish_block(q)
        else:
            mix(q)

    waiting = []
    done = 0
    opened = False
    for code in ORDER:
        if code < 0:
            q, n = divmod(-code - 1, 15)
            hop(q, NODES[n]).start()
            continue
        if code >= OUTER:
            (sum_raw, spread_total, update)[code - OUTER]()
            continue
        if not opened:
            opened = True
            for step in (1, 2, 3):
                raw_send(step).start()
            for o in range(CHIPS):
                feat_send(o).start()
            q_copy.start()
            g_copy.start()
            m_copy.start()
            row = lax.broadcast_in_dim(segs[...], (ROWS, ROWS), (0, 1))
            t_at = lax.broadcasted_iota(jnp.int32, (ROWS, ROWS), 0)
            s_at = lax.broadcasted_iota(jnp.int32, (ROWS, ROWS), 1)
            allowed = (row == row.T) & (s_at <= t_at)
            bias[...] = jnp.where(allowed, 0.0, -1e30)
        q, n = divmod(code, 15)
        arrive(q, NODES[n])
        for child in NODES:
            if TREES[q][child] == NODES[n]:
                hop(q, child).start()
        done += 1
        pending[q].append(NODES[n])
        left[q] -= 1
        if not state["ready"] and done >= 4:
            state["ready"] = True
            for o in own_weights:
                o.wait()
            view = feats.at[:, pl.ds(pl.multiple_of(c * ROWS, ROWS), ROWS)]
            pltpu.make_async_copy(view, view, feat_sem).wait()
            all_feats(other).wait_recv()
            for qq in range(NQ):
                pending[qq].append((0, 0))
        if state["ready"] and (len(pending[q]) >= GROUP or left[q] == 0 or done > TAIL):
            flush(q)
        for item in list(waiting):
            if done >= item[0] + 2 and (item[1] < 2 or not todo):
                waiting.remove(item)
                settle(item[1])
        if left[q] == 0:
            exchange(q).start()
            waiting.append((done, q))
        remaining = len(RECEIVES) - done
        if todo:
            count = -(-len(todo) // max(1, remaining - 3))
            for start in todo[:count]:
                softmax_heads(start)
            del todo[:count]

    for start in todo:
        softmax_heads(start)
    for _, q in waiting:
        settle(q)

    for q in range(NQ):
        for child in NODES:
            hop(q, child).wait_send()
        exchange(q).wait_send()
    all_feats(other).wait_send()
    for step in (1, 2, 3):
        raw_send(step).wait_send()
        spread(step).wait_send()


def finish_kernel(
    mixed, late_probs, late_values, gv, mv, attended, new_params, new_moment, late_mixed, early_sem, late_sem, p_sem, m_sem
):
    half = 2 * Q_GROUP * HD
    piece = Q_GROUP * HD
    early = pltpu.make_async_copy(mixed, attended.at[:, pl.ds((1 - LATE) * half, half)], early_sem)
    copies = [early, pltpu.make_async_copy(gv, new_params, p_sem), pltpu.make_async_copy(mv, new_moment, m_sem)]
    for copy in copies:
        copy.start()
    for j in range(2):
        values = late_values[:, j * HD : (j + 1) * HD]
        for i in range(Q_GROUP):
            h = j * Q_GROUP + i
            out = jnp.dot(late_probs[h], values, preferred_element_type=jnp.float32)
            late_mixed[:, h * HD : (h + 1) * HD] = out.astype(jnp.bfloat16)
        copy = pltpu.make_async_copy(
            late_mixed.at[:, pl.ds(j * piece, piece)],
            attended.at[:, pl.ds(LATE * half + j * piece, piece)],
            late_sem.at[j],
        )
        copy.start()
        copies.append(copy)
    for copy in copies:
        copy.wait()


def shards(tokens, queries, segments, local_weights, global_params, momentum):
    hbm = pl.BlockSpec(memory_space=pltpu.HBM)
    any_space = pl.BlockSpec(memory_space=pl.ANY)
    vmem = pl.BlockSpec(memory_space=pltpu.VMEM)
    dma = pltpu.SemaphoreType.DMA
    half = 2 * Q_GROUP
    kept = pl.pallas_call(
        kernel,
        out_shape=(
            pltpu.VMEM((ROWS, half * HD), jnp.bfloat16),
            pltpu.VMEM((half, ROWS, ROWS), jnp.bfloat16),
            pltpu.VMEM((ROWS, BLK), jnp.bfloat16),
            pltpu.VMEM((ROWS, KVW), jnp.float32),
            pltpu.VMEM((ROWS, KVW), jnp.float32),
        ),
        in_specs=[hbm, hbm, vmem, hbm, hbm, hbm],
        out_specs=(vmem,) * 5,
        scratch_shapes=[
            pltpu.VMEM((CHIPS, NQ, BLK, BLK), jnp.bfloat16),
            pltpu.VMEM((CHIPS, 2 * ROWS, BLK), jnp.bfloat16),
            pltpu.VMEM((NQ, 2 * ROWS, BLK), jnp.float32),
            pltpu.VMEM((NQ, ROWS, BLK), jnp.float32),
            pltpu.VMEM((ROWS, QH * HD), jnp.bfloat16),
            pltpu.VMEM((ROWS, ROWS), jnp.float32),
            pltpu.VMEM((half, ROWS, ROWS), jnp.bfloat16),
            pltpu.VMEM((ROWS, 2 * BLK), jnp.bfloat16),
            pltpu.VMEM((X, PART, KVW), jnp.bfloat16),
            pltpu.VMEM((PART, KVW), jnp.float32),
            pltpu.VMEM((PART, KVW), jnp.float32),
            pltpu.VMEM((X, PART, KVW), jnp.float32),
            dma((NQ, 15)), dma((NQ, 15)), dma, dma, dma((3,)), dma((3,)), dma, dma, dma((3,)), dma((3,)),
            dma((NQ,)), dma((NQ,)),
            dma((NQ,)), dma, dma, dma, dma, dma,
        ],
        compiler_params=pltpu.CompilerParams(
            collective_id=0, has_side_effects=True, vmem_limit_bytes=57 * 2**20
        ),
        cost_estimate=pl.CostEstimate(flops=6 * 10**9, bytes_accessed=13 * 2**20, transcendentals=2**21),
        name="sync_and_attend",
    )(tokens[0], queries[0], segments[0], local_weights[0], global_params, momentum)
    attended, new_params, new_momentum = pl.pallas_call(
        finish_kernel,
        out_shape=(
            jax.ShapeDtypeStruct((ROWS, QH * HD), jnp.bfloat16),
            jax.ShapeDtypeStruct((ROWS, KVW), jnp.float32),
            jax.ShapeDtypeStruct((ROWS, KVW), jnp.float32),
        ),
        in_specs=[vmem] * 5,
        out_specs=(any_space,) * 3,
        scratch_shapes=[pltpu.VMEM((ROWS, half * HD), jnp.bfloat16), dma, dma((2,)), dma, dma],
        compiler_params=pltpu.CompilerParams(vmem_limit_bytes=16 * 2**20),
        name="finish",
    )(*kept)
    return (attended[None], new_params, new_momentum)


def solution(mesh):
    placed = (
        P("replica", "fsdp", None),
        P("replica", "fsdp", None),
        P("replica", "fsdp", None),
        P("replica", "fsdp", None),
        P("fsdp", None),
        P("fsdp", None),
    )
    return jax.shard_map(
        shards,
        mesh=mesh,
        in_specs=placed,
        out_specs=(P("replica", "fsdp", None), P("fsdp", None), P("fsdp", None)),
        check_vma=False,
    )
```

```python
import math

import jax
import jax.numpy as jnp
from jax import lax
from jax.experimental import pallas as pl
from jax.experimental.pallas import tpu as pltpu
from jax.sharding import PartitionSpec as P

HD = 128
QH = 32
Q_GROUP = 8
ROWS = 256
WIDTH = 8192
KVW = 1024
BLK = 256
NQ = KVW // BLK
CHIPS = 16
X = 4
PART = ROWS // X
MESH = pl.DeviceIdType.MESH

NODES = (
    (0, 1), (0, -1), (1, 0), (-1, 0), (2, 0),
    (1, 1), (-1, 1), (1, -1), (-1, -1), (0, 2),
    (2, 1), (2, -1), (1, 2), (-1, 2), (2, 2),
)
PARENTS = {
    (0, 1): (0, 0), (0, -1): (0, 0), (1, 0): (0, 0), (-1, 0): (0, 0), (2, 0): (1, 0),
    (1, 1): (0, 1), (-1, 1): (0, 1), (1, -1): (0, -1), (-1, -1): (0, -1), (0, 2): (0, 1),
    (2, 1): (-1, 1), (2, -1): (1, -1), (1, 2): (1, 1), (-1, 2): (-1, -1), (2, 2): (-1, 2),
}
TREES = (PARENTS | {(-1, 2): (0, 2)}, PARENTS | {(1, 2): (0, 2)}, PARENTS, PARENTS)
ORDER = (
    -18, -17, -49, -16, -2, -4, -48, -1, -34, -19, -31, -33, -3, 15, 32,
    16, 0, 21, -47, 33, 23, 1, -32, 100, 17, 6, 22, 20, 34, 24,
    -46, 18, 30, 8, 46, 28, 31, 2, 9, 26, 48, 25, 53, 19, 29,
    27, 36, 5, 38, 45, 10, 13, 39, 7, 101, 40, 47, 58, 3, 52,
    50, 37, 35, 12, 4, 51, 11, 14, 43, 54, 49, 56, 55, 57, 41,
    59, 44, 42, 102,
)
GROUP = 4
RECEIVES = [code for code in ORDER if 0 <= code < 100]
OUTER = 100
TAIL = 55
LATE = RECEIVES[-1] // 15 - 2


def kernel(
    tokens, queries, segs, weights, params, moment,
    mixed, late_probs, late_values, gv, mv,
    gathered, feats, acc, incoming, qv, bias, probs, keys,
    raw, partsum, partin, total,
    gsend, grecv, tsend, trecv, xsend, xrecv, zsend, zrecv, bsend, brecv, psend, precv,
    own_sem, feat_sem, q_sem, raw_sem, g_sem, m_sem,
):
    r = lax.axis_index("replica")
    f = lax.axis_index("fsdp")
    zl, x = r // X, r % X
    y, zh, c = f // 8, (f // 2) % 4, f % 2
    sign = 1 - 2 * c
    other = 1 - c
    sibling = (r, f + 1 - 2 * c)
    zpeer = ((1 - zl) * X + x, f)

    def xpeer(step):
        return (zl * X + (x + step) % X, f)

    def dev(dy, dz):
        return (r, (((y + dy + 4) % 4) * 4 + (zh + dz * sign + 4) % 4) * 2 + c)

    def slot(node):
        return ((y - node[0] + 4) % 4) * 4 + (zh - node[1] * sign + 4) % 4

    own = y * 4 + zh

    own_feats = [
        pltpu.make_async_copy(
            tokens.at[:, pl.ds(pl.multiple_of((2 * o + c) * BLK, BLK), BLK)],
            feats.at[o, pl.ds(pl.multiple_of(c * ROWS, ROWS), ROWS)],
            feat_sem,
        )
        for o in range(CHIPS)
    ]
    own_weights = [
        pltpu.make_async_copy(weights.at[:, pl.ds(q * BLK, BLK)], gathered.at[own, q], own_sem.at[q])
        for q in range(NQ)
    ]
    q_copy = pltpu.make_async_copy(queries, qv, q_sem)
    g_copy = pltpu.make_async_copy(params, gv, g_sem)
    m_copy = pltpu.make_async_copy(moment, mv, m_sem)
    raw_copy = pltpu.make_async_copy(weights.at[pl.ds(pl.multiple_of(x * PART, PART), PART)], raw.at[x], raw_sem)

    barrier = pltpu.get_barrier_semaphore()
    peers = [dev(1, 0), dev(-1, 0), dev(0, 1), dev(0, -1), sibling, zpeer, xpeer(1), xpeer(2), xpeer(3)]
    for peer in peers:
        pl.semaphore_signal(barrier, inc=1, device_id=peer, device_id_type=MESH)
    for copy in own_weights + own_feats:
        copy.start()
    raw_copy.start()
    pl.semaphore_wait(barrier, len(peers))

    def hop(q, child):
        node = TREES[q][child]
        at, index = slot(node), NODES.index(child)
        source = weights.at[:, pl.ds(q * BLK, BLK)] if node == (0, 0) else gathered.at[at, q]
        return pltpu.make_async_remote_copy(
            src_ref=source, dst_ref=gathered.at[at, q],
            send_sem=gsend, recv_sem=grecv.at[q, index],
            device_id=dev(*step_of(q, child)), device_id_type=MESH,
        )

    def step_of(q, child):
        node = TREES[q][child]
        dy, dz = (child[0] - node[0]) % 4, (child[1] - node[1]) % 4
        return (dy - 4 if dy == 3 else dy, dz - 4 if dz == 3 else dz)

    def arrive(q, node):
        at, index = slot(node), NODES.index(node)
        pltpu.make_async_remote_copy(
            src_ref=gathered.at[at, q], dst_ref=gathered.at[at, q],
            send_sem=gsend, recv_sem=grecv.at[q, index],
            device_id=sibling, device_id_type=MESH,
        ).wait_recv()

    def feat_send(o):
        return pltpu.make_async_remote_copy(
            src_ref=tokens.at[:, pl.ds(pl.multiple_of((2 * o + other) * BLK, BLK), BLK)],
            dst_ref=feats.at[o, pl.ds(pl.multiple_of(c * ROWS, ROWS), ROWS)],
            send_sem=tsend, recv_sem=trecv, device_id=sibling, device_id_type=MESH,
        )

    def all_feats(row_core):
        view = feats.at[:, pl.ds(pl.multiple_of(row_core * ROWS, ROWS), ROWS)]
        return pltpu.make_async_remote_copy(
            src_ref=view, dst_ref=view, send_sem=tsend, recv_sem=trecv, device_id=sibling, device_id_type=MESH
        )

    def raw_send(step):
        to = (x + step) % X
        return pltpu.make_async_remote_copy(
            src_ref=weights.at[pl.ds(pl.multiple_of(to * PART, PART), PART)], dst_ref=raw.at[x],
            send_sem=xsend.at[step - 1], recv_sem=xrecv.at[step - 1], device_id=xpeer(step), device_id_type=MESH,
        )

    def raw_arrive(step):
        at = (x - step + X) % X
        pltpu.make_async_remote_copy(
            src_ref=raw.at[at], dst_ref=raw.at[at],
            send_sem=xsend.at[step - 1], recv_sem=xrecv.at[step - 1], device_id=xpeer(step), device_id_type=MESH,
        ).wait_recv()

    z_copy = pltpu.make_async_remote_copy(
        src_ref=partsum, dst_ref=partin, send_sem=zsend, recv_sem=zrecv, device_id=zpeer, device_id_type=MESH
    )

    def spread(step):
        return pltpu.make_async_remote_copy(
            src_ref=total.at[x], dst_ref=total.at[x],
            send_sem=bsend.at[step - 1], recv_sem=brecv.at[step - 1], device_id=xpeer(step), device_id_type=MESH,
        )

    def spread_arrive(step):
        at = (x - step + X) % X
        pltpu.make_async_remote_copy(
            src_ref=total.at[at], dst_ref=total.at[at],
            send_sem=bsend.at[step - 1], recv_sem=brecv.at[step - 1], device_id=xpeer(step), device_id_type=MESH,
        ).wait_recv()

    def exchange(q):
        return pltpu.make_async_remote_copy(
            src_ref=acc.at[q, pl.ds(pl.multiple_of(other * ROWS, ROWS), ROWS)], dst_ref=incoming.at[q],
            send_sem=psend.at[q], recv_sem=precv.at[q], device_id=sibling, device_id_type=MESH,
        )

    def multiply(q, nodes, fresh=False):
        partial = None
        for s in [slot(node) for node in nodes]:
            term = jnp.dot(feats[s], gathered[s, q], preferred_element_type=jnp.float32)
            partial = term if partial is None else partial + term
        acc[q] = partial if fresh else acc[q] + partial

    def finish_block(q):
        mine = acc[q, pl.ds(pl.multiple_of(c * ROWS, ROWS), ROWS), :]
        return ((mine + incoming[q]) * WIDTH ** (-0.5)).astype(jnp.bfloat16)

    def softmax_heads(start):
        kv = start // Q_GROUP
        target = late_probs if start // (2 * Q_GROUP) == LATE else probs
        for h in range(start, start + 2):
            scores = lax.dot_general(
                qv[:, h * HD : (h + 1) * HD], keys[:, kv * HD : (kv + 1) * HD],
                (((1,), (1,)), ((), ())), preferred_element_type=jnp.float32,
            )
            scores = scores * (HD ** (-0.5) * math.log2(math.e)) + bias[...]
            top = jnp.max(scores, axis=1, keepdims=True)
            weight = jnp.exp2(scores - top)
            norm = 1.0 / jnp.sum(weight, axis=1, keepdims=True)
            target[h % (2 * Q_GROUP)] = (weight * norm).astype(jnp.bfloat16)

    def mix(q):
        block = finish_block(q)
        for j in range(2):
            values = block[:, j * HD : (j + 1) * HD]

            for h in range(j * Q_GROUP, (j + 1) * Q_GROUP):
                out = jnp.dot(probs[h], values, preferred_element_type=jnp.float32)
                mixed[:, h * HD : (h + 1) * HD] = out.astype(jnp.bfloat16)

    def sum_raw():
        for step in (1, 2, 3):
            raw_arrive(step)
        raw_copy.wait()
        partsum[...] = (
            raw[0].astype(jnp.float32) + raw[1].astype(jnp.float32) + raw[2].astype(jnp.float32) + raw[3].astype(jnp.float32)
        )
        z_copy.start()

    def spread_total():
        z_copy.wait()
        total[x] = partsum[...] + partin[...]
        for step in (1, 2, 3):
            spread(step).start()

    def update():
        for step in (1, 2, 3):
            spread_arrive(step)
        g_copy.wait()
        m_copy.wait()

        @pl.loop(0, X)
        def _(j):
            at = pl.ds(pl.multiple_of(j * PART, PART), PART)
            g = gv[at, :]
            grad = g - total[j] * 0.125
            fresh = 0.9 * mv[at, :] + grad
            mv[at, :] = fresh
            gv[at, :] = g - 0.7 * (grad + 0.9 * fresh)

    pending = {q: [] for q in range(NQ)}
    left = {q: CHIPS - 1 for q in range(NQ)}
    started = set()
    todo = []
    state = {"ready": False, "queries": False}

    def flush(q):
        if pending[q]:
            multiply(q, pending[q], fresh=q not in started)
            started.add(q)
            pending[q] = []

    def settle(q):
        exchange(q).wait_recv()
        if q < 2:
            keys[:, q * BLK : (q + 1) * BLK] = finish_block(q)
            if not state["queries"]:
                state["queries"] = True
                q_copy.wait()
            todo.extend(range(q * 2 * Q_GROUP, (q + 1) * 2 * Q_GROUP, 2))
        elif q - 2 == LATE:
            late_values[...] = finish_block(q)
        else:
            mix(q)

    waiting = []
    done = 0
    opened = False
    for code in ORDER:
        if code < 0:
            q, n = divmod(-code - 1, 15)
            hop(q, NODES[n]).start()
            continue
        if code >= OUTER:
            (sum_raw, spread_total, update)[code - OUTER]()
            continue
        if not opened:
            opened = True
            for step in (1, 2, 3):
                raw_send(step).start()
            for o in range(CHIPS):
                feat_send(o).start()
            q_copy.start()
            g_copy.start()
            m_copy.start()
            row = lax.broadcast_in_dim(segs[...], (ROWS, ROWS), (0, 1))
            t_at = lax.broadcasted_iota(jnp.int32, (ROWS, ROWS), 0)
            s_at = lax.broadcasted_iota(jnp.int32, (ROWS, ROWS), 1)
            allowed = (row == row.T) & (s_at <= t_at)
            bias[...] = jnp.where(allowed, 0.0, -1e30)
        q, n = divmod(code, 15)
        arrive(q, NODES[n])
        for child in NODES:
            if TREES[q][child] == NODES[n]:
                hop(q, child).start()
        done += 1
        pending[q].append(NODES[n])
        left[q] -= 1
        if not state["ready"] and done >= 4:
            state["ready"] = True
            for o in own_weights:
                o.wait()
            view = feats.at[:, pl.ds(pl.multiple_of(c * ROWS, ROWS), ROWS)]
            pltpu.make_async_copy(view, view, feat_sem).wait()
            all_feats(other).wait_recv()
            for qq in range(NQ):
                pending[qq].append((0, 0))
        if state["ready"] and (len(pending[q]) >= GROUP or left[q] == 0 or done > TAIL):
            flush(q)
        for item in list(waiting):
            if done >= item[0] + 2 and (item[1] < 2 or not todo):
                waiting.remove(item)
                settle(item[1])
        if left[q] == 0:
            exchange(q).start()
            waiting.append((done, q))
        remaining = len(RECEIVES) - done
        if todo:
            count = -(-len(todo) // max(1, remaining - 3))
            for start in todo[:count]:
                softmax_heads(start)
            del todo[:count]

    for start in todo:
        softmax_heads(start)
    sent = gathered.at[pl.ds(0, CHIPS - 1)]
    pltpu.make_async_remote_copy(
        src_ref=sent, dst_ref=sent, send_sem=gsend, recv_sem=trecv, device_id=sibling, device_id_type=MESH
    ).wait_send()
    all_feats(other).wait_send()
    for step in (1, 2, 3):
        raw_send(step).wait_send()
        spread(step).wait_send()
    for _, q in waiting:
        settle(q)
    for q in range(NQ):
        exchange(q).wait_send()


def finish_kernel(
    mixed, late_probs, late_values, gv, mv, attended, new_params, new_moment, late_mixed, early_sem, late_sem, p_sem, m_sem
):
    half = 2 * Q_GROUP * HD
    piece = Q_GROUP * HD
    early = pltpu.make_async_copy(mixed, attended.at[:, pl.ds((1 - LATE) * half, half)], early_sem)
    copies = [early, pltpu.make_async_copy(gv, new_params, p_sem), pltpu.make_async_copy(mv, new_moment, m_sem)]
    for copy in copies:
        copy.start()
    for j in range(2):
        values = late_values[:, j * HD : (j + 1) * HD]
        for i in range(Q_GROUP):
            h = j * Q_GROUP + i
            out = jnp.dot(late_probs[h], values, preferred_element_type=jnp.float32)
            late_mixed[:, h * HD : (h + 1) * HD] = out.astype(jnp.bfloat16)
        copy = pltpu.make_async_copy(
            late_mixed.at[:, pl.ds(j * piece, piece)],
            attended.at[:, pl.ds(LATE * half + j * piece, piece)],
            late_sem.at[j],
        )
        copy.start()
        copies.append(copy)
    for copy in copies:
        copy.wait()


def shards(tokens, queries, segments, local_weights, global_params, momentum):
    hbm = pl.BlockSpec(memory_space=pltpu.HBM)
    any_space = pl.BlockSpec(memory_space=pl.ANY)
    vmem = pl.BlockSpec(memory_space=pltpu.VMEM)
    dma = pltpu.SemaphoreType.DMA
    half = 2 * Q_GROUP
    kept = pl.pallas_call(
        kernel,
        out_shape=(
            pltpu.VMEM((ROWS, half * HD), jnp.bfloat16),
            pltpu.VMEM((half, ROWS, ROWS), jnp.bfloat16),
            pltpu.VMEM((ROWS, BLK), jnp.bfloat16),
            pltpu.VMEM((ROWS, KVW), jnp.float32),
            pltpu.VMEM((ROWS, KVW), jnp.float32),
        ),
        in_specs=[hbm, hbm, vmem, hbm, hbm, hbm],
        out_specs=(vmem,) * 5,
        scratch_shapes=[
            pltpu.VMEM((CHIPS, NQ, BLK, BLK), jnp.bfloat16),
            pltpu.VMEM((CHIPS, 2 * ROWS, BLK), jnp.bfloat16),
            pltpu.VMEM((NQ, 2 * ROWS, BLK), jnp.float32),
            pltpu.VMEM((NQ, ROWS, BLK), jnp.float32),
            pltpu.VMEM((ROWS, QH * HD), jnp.bfloat16),
            pltpu.VMEM((ROWS, ROWS), jnp.float32),
            pltpu.VMEM((half, ROWS, ROWS), jnp.bfloat16),
            pltpu.VMEM((ROWS, 2 * BLK), jnp.bfloat16),
            pltpu.VMEM((X, PART, KVW), jnp.bfloat16),
            pltpu.VMEM((PART, KVW), jnp.float32),
            pltpu.VMEM((PART, KVW), jnp.float32),
            pltpu.VMEM((X, PART, KVW), jnp.float32),
            dma, dma((NQ, 15)), dma, dma, dma((3,)), dma((3,)), dma, dma, dma((3,)), dma((3,)),
            dma((NQ,)), dma((NQ,)),
            dma((NQ,)), dma, dma, dma, dma, dma,
        ],
        compiler_params=pltpu.CompilerParams(
            collective_id=0, has_side_effects=True, vmem_limit_bytes=57 * 2**20
        ),
        cost_estimate=pl.CostEstimate(flops=6 * 10**9, bytes_accessed=13 * 2**20, transcendentals=2**21),
        name="sync_and_attend",
    )(tokens[0], queries[0], segments[0], local_weights[0], global_params, momentum)
    attended, new_params, new_momentum = pl.pallas_call(
        finish_kernel,
        out_shape=(
            jax.ShapeDtypeStruct((ROWS, QH * HD), jnp.bfloat16),
            jax.ShapeDtypeStruct((ROWS, KVW), jnp.float32),
            jax.ShapeDtypeStruct((ROWS, KVW), jnp.float32),
        ),
        in_specs=[vmem] * 5,
        out_specs=(any_space,) * 3,
        scratch_shapes=[pltpu.VMEM((ROWS, half * HD), jnp.bfloat16), dma, dma((2,)), dma, dma],
        compiler_params=pltpu.CompilerParams(vmem_limit_bytes=16 * 2**20),
        name="finish",
    )(*kept)
    return (attended[None], new_params, new_momentum)


def solution(mesh):
    placed = (
        P("replica", "fsdp", None),
        P("replica", "fsdp", None),
        P("replica", "fsdp", None),
        P("replica", "fsdp", None),
        P("fsdp", None),
        P("fsdp", None),
    )
    return jax.shard_map(
        shards,
        mesh=mesh,
        in_specs=placed,
        out_specs=(P("replica", "fsdp", None), P("fsdp", None), P("fsdp", None)),
        check_vma=False,
    )
```

```python
import math

import jax
import jax.numpy as jnp
from jax import lax
from jax.experimental import pallas as pl
from jax.experimental.pallas import tpu as pltpu
from jax.sharding import PartitionSpec as P

HD = 128
QH = 32
Q_GROUP = 8
ROWS = 256
WIDTH = 8192
KVW = 1024
BLK = 256
NQ = KVW // BLK
CHIPS = 16
X = 4
PART = ROWS // X
MESH = pl.DeviceIdType.MESH

NODES = (
    (0, 1), (0, -1), (1, 0), (-1, 0), (2, 0),
    (1, 1), (-1, 1), (1, -1), (-1, -1), (0, 2),
    (2, 1), (2, -1), (1, 2), (-1, 2), (2, 2),
)
PARENTS = {
    (0, 1): (0, 0), (0, -1): (0, 0), (1, 0): (0, 0), (-1, 0): (0, 0), (2, 0): (1, 0),
    (1, 1): (0, 1), (-1, 1): (0, 1), (1, -1): (0, -1), (-1, -1): (0, -1), (0, 2): (0, 1),
    (2, 1): (-1, 1), (2, -1): (1, -1), (1, 2): (1, 1), (-1, 2): (-1, -1), (2, 2): (-1, 2),
}
TREES = (PARENTS | {(-1, 2): (0, 2)}, PARENTS | {(1, 2): (0, 2)}, PARENTS, PARENTS)
ORDER = (
    -18, -17, -49, -16, -2, -4, -48, -1, -34, -19, -31, -33, -3, 15, 32,
    16, 0, 21, -47, 33, 23, 1, -32, 100, 17, 6, 22, 20, 34, 24,
    -46, 18, 30, 8, 46, 28, 31, 2, 9, 26, 48, 25, 53, 19, 29,
    27, 36, 5, 38, 45, 10, 13, 39, 7, 101, 40, 47, 58, 3, 52,
    50, 37, 35, 12, 4, 51, 11, 14, 43, 54, 49, 56, 55, 57, 41,
    59, 44, 42, 102,
)
GROUP = 4
RECEIVES = [code for code in ORDER if 0 <= code < 100]
OUTER = 100
TAIL = 55
LATE = RECEIVES[-1] // 15 - 2


def kernel(
    tokens, queries, segs, weights, params, moment,
    mixed, late_probs, late_values, gv, mv,
    gathered, feats, acc, incoming, qv, bias, probs, keys,
    raw, partsum, partin, total,
    gsend, grecv, tsend, trecv, xsend, xrecv, zsend, zrecv, bsend, brecv, psend, precv,
    own_sem, feat_sem, q_sem, raw_sem, g_sem, m_sem,
):
    r = lax.axis_index("replica")
    f = lax.axis_index("fsdp")
    zl, x = r // X, r % X
    y, zh, c = f // 8, (f // 2) % 4, f % 2
    sign = 1 - 2 * c
    other = 1 - c
    sibling = (r, f + 1 - 2 * c)
    zpeer = ((1 - zl) * X + x, f)

    def xpeer(step):
        return (zl * X + (x + step) % X, f)

    def dev(dy, dz):
        return (r, (((y + dy + 4) % 4) * 4 + (zh + dz * sign + 4) % 4) * 2 + c)

    def slot(node):
        return ((y - node[0] + 4) % 4) * 4 + (zh - node[1] * sign + 4) % 4

    own = y * 4 + zh

    own_feats = [
        pltpu.make_async_copy(
            tokens.at[:, pl.ds(pl.multiple_of((2 * o + c) * BLK, BLK), BLK)],
            feats.at[o, pl.ds(pl.multiple_of(c * ROWS, ROWS), ROWS)],
            feat_sem,
        )
        for o in range(CHIPS)
    ]
    own_weights = [
        pltpu.make_async_copy(weights.at[:, pl.ds(q * BLK, BLK)], gathered.at[own, q], own_sem.at[q])
        for q in range(NQ)
    ]
    q_copy = pltpu.make_async_copy(queries, qv, q_sem)
    g_copy = pltpu.make_async_copy(params, gv, g_sem)
    m_copy = pltpu.make_async_copy(moment, mv, m_sem)
    raw_copy = pltpu.make_async_copy(weights.at[pl.ds(pl.multiple_of(x * PART, PART), PART)], raw.at[x], raw_sem)

    barrier = pltpu.get_barrier_semaphore()
    peers = [dev(1, 0), dev(-1, 0), dev(0, 1), dev(0, -1), sibling, zpeer, xpeer(1), xpeer(2), xpeer(3)]
    for peer in peers:
        pl.semaphore_signal(barrier, inc=1, device_id=peer, device_id_type=MESH)
    for copy in own_weights + own_feats:
        copy.start()
    raw_copy.start()
    pl.semaphore_wait(barrier, len(peers))

    def hop(q, child):
        node = TREES[q][child]
        at, index = slot(node), NODES.index(child)
        source = weights.at[:, pl.ds(q * BLK, BLK)] if node == (0, 0) else gathered.at[at, q]
        return pltpu.make_async_remote_copy(
            src_ref=source, dst_ref=gathered.at[at, q],
            send_sem=gsend, recv_sem=grecv.at[q, index],
            device_id=dev(*step_of(q, child)), device_id_type=MESH,
        )

    def step_of(q, child):
        node = TREES[q][child]
        dy, dz = (child[0] - node[0]) % 4, (child[1] - node[1]) % 4
        return (dy - 4 if dy == 3 else dy, dz - 4 if dz == 3 else dz)

    def arrive(q, node):
        at, index = slot(node), NODES.index(node)
        pltpu.make_async_remote_copy(
            src_ref=gathered.at[at, q], dst_ref=gathered.at[at, q],
            send_sem=gsend, recv_sem=grecv.at[q, index],
            device_id=sibling, device_id_type=MESH,
        ).wait_recv()

    def feat_send(o):
        return pltpu.make_async_remote_copy(
            src_ref=tokens.at[:, pl.ds(pl.multiple_of((2 * o + other) * BLK, BLK), BLK)],
            dst_ref=feats.at[o, pl.ds(pl.multiple_of(c * ROWS, ROWS), ROWS)],
            send_sem=tsend, recv_sem=trecv, device_id=sibling, device_id_type=MESH,
        )

    def all_feats(row_core):
        view = feats.at[:, pl.ds(pl.multiple_of(row_core * ROWS, ROWS), ROWS)]
        return pltpu.make_async_remote_copy(
            src_ref=view, dst_ref=view, send_sem=tsend, recv_sem=trecv, device_id=sibling, device_id_type=MESH
        )

    def raw_send(step):
        to = (x + step) % X
        return pltpu.make_async_remote_copy(
            src_ref=weights.at[pl.ds(pl.multiple_of(to * PART, PART), PART)], dst_ref=raw.at[x],
            send_sem=xsend.at[step - 1], recv_sem=xrecv.at[step - 1], device_id=xpeer(step), device_id_type=MESH,
        )

    def raw_arrive(step):
        at = (x - step + X) % X
        pltpu.make_async_remote_copy(
            src_ref=raw.at[at], dst_ref=raw.at[at],
            send_sem=xsend.at[step - 1], recv_sem=xrecv.at[step - 1], device_id=xpeer(step), device_id_type=MESH,
        ).wait_recv()

    z_copy = pltpu.make_async_remote_copy(
        src_ref=partsum, dst_ref=partin, send_sem=zsend, recv_sem=zrecv, device_id=zpeer, device_id_type=MESH
    )

    def spread(step):
        return pltpu.make_async_remote_copy(
            src_ref=total.at[x], dst_ref=total.at[x],
            send_sem=bsend.at[step - 1], recv_sem=brecv.at[step - 1], device_id=xpeer(step), device_id_type=MESH,
        )

    def spread_arrive(step):
        at = (x - step + X) % X
        pltpu.make_async_remote_copy(
            src_ref=total.at[at], dst_ref=total.at[at],
            send_sem=bsend.at[step - 1], recv_sem=brecv.at[step - 1], device_id=xpeer(step), device_id_type=MESH,
        ).wait_recv()

    def exchange(q):
        return pltpu.make_async_remote_copy(
            src_ref=acc.at[q, pl.ds(pl.multiple_of(other * ROWS, ROWS), ROWS)], dst_ref=incoming.at[q],
            send_sem=psend.at[q], recv_sem=precv.at[q], device_id=sibling, device_id_type=MESH,
        )

    def multiply(q, nodes, fresh=False):
        partial = None
        for s in [slot(node) for node in nodes]:
            term = jnp.dot(feats[s], gathered[s, q], preferred_element_type=jnp.float32)
            partial = term if partial is None else partial + term
        acc[q] = partial if fresh else acc[q] + partial

    def finish_block(q):
        mine = acc[q, pl.ds(pl.multiple_of(c * ROWS, ROWS), ROWS), :]
        return ((mine + incoming[q]) * WIDTH ** (-0.5)).astype(jnp.bfloat16)

    def softmax_heads(start):
        kv = start // Q_GROUP
        target = late_probs if start // (2 * Q_GROUP) == LATE else probs
        for h in range(start, start + 2):
            scores = lax.dot_general(
                qv[:, h * HD : (h + 1) * HD], keys[:, kv * HD : (kv + 1) * HD],
                (((1,), (1,)), ((), ())), preferred_element_type=jnp.float32,
            )
            scores = scores * (HD ** (-0.5) * math.log2(math.e)) + bias[...]
            top = jnp.max(scores, axis=1, keepdims=True)
            weight = jnp.exp2(scores - top)
            norm = 1.0 / jnp.sum(weight, axis=1, keepdims=True)
            target[h % (2 * Q_GROUP)] = (weight * norm).astype(jnp.bfloat16)

    def mix(q):
        block = finish_block(q)
        for j in range(2):
            values = block[:, j * HD : (j + 1) * HD]

            for h in range(j * Q_GROUP, (j + 1) * Q_GROUP):
                out = jnp.dot(probs[h], values, preferred_element_type=jnp.float32)
                mixed[:, h * HD : (h + 1) * HD] = out.astype(jnp.bfloat16)

    def sum_raw():
        for step in (1, 2, 3):
            raw_arrive(step)
        raw_copy.wait()
        partsum[...] = (
            raw[0].astype(jnp.float32) + raw[1].astype(jnp.float32) + raw[2].astype(jnp.float32) + raw[3].astype(jnp.float32)
        )
        z_copy.start()

    def spread_total():
        z_copy.wait()
        total[x] = partsum[...] + partin[...]
        for step in (1, 2, 3):
            spread(step).start()

    def update():
        for step in (1, 2, 3):
            spread_arrive(step)
        g_copy.wait()
        m_copy.wait()

        @pl.loop(0, X)
        def _(j):
            at = pl.ds(pl.multiple_of(j * PART, PART), PART)
            g = gv[at, :]
            grad = g - total[j] * 0.125
            fresh = 0.9 * mv[at, :] + grad
            mv[at, :] = fresh
            gv[at, :] = g - 0.7 * (grad + 0.9 * fresh)

    pending = {q: [] for q in range(NQ)}
    left = {q: CHIPS - 1 for q in range(NQ)}
    started = set()
    todo = []
    state = {"ready": False, "queries": False}

    def flush(q):
        if pending[q]:
            multiply(q, pending[q], fresh=q not in started)
            started.add(q)
            pending[q] = []

    def settle(q):
        exchange(q).wait_recv()
        if q < 2:
            keys[:, q * BLK : (q + 1) * BLK] = finish_block(q)
            if not state["queries"]:
                state["queries"] = True
                q_copy.wait()
            todo.extend(range(q * 2 * Q_GROUP, (q + 1) * 2 * Q_GROUP, 2))
        elif q - 2 == LATE:
            late_values[...] = finish_block(q)
        else:
            mix(q)

    waiting = []
    done = 0
    opened = False
    for code in ORDER:
        if code < 0:
            q, n = divmod(-code - 1, 15)
            hop(q, NODES[n]).start()
            continue
        if code >= OUTER:
            (sum_raw, spread_total, update)[code - OUTER]()
            continue
        if not opened:
            opened = True
            for step in (1, 2, 3):
                raw_send(step).start()
            for o in range(CHIPS):
                feat_send(o).start()
            q_copy.start()
            g_copy.start()
            m_copy.start()
            row = lax.broadcast_in_dim(segs[...], (ROWS, ROWS), (0, 1))
            t_at = lax.broadcasted_iota(jnp.int32, (ROWS, ROWS), 0)
            s_at = lax.broadcasted_iota(jnp.int32, (ROWS, ROWS), 1)
            allowed = (row == row.T) & (s_at <= t_at)
            bias[...] = jnp.where(allowed, 0.0, -1e30)
        q, n = divmod(code, 15)
        arrive(q, NODES[n])
        for child in NODES:
            if TREES[q][child] == NODES[n]:
                hop(q, child).start()
        done += 1
        pending[q].append(NODES[n])
        left[q] -= 1
        if not state["ready"] and done >= 4:
            state["ready"] = True
            for o in own_weights:
                o.wait()
            view = feats.at[:, pl.ds(pl.multiple_of(c * ROWS, ROWS), ROWS)]
            pltpu.make_async_copy(view, view, feat_sem).wait()
            all_feats(other).wait_recv()
            for qq in range(NQ):
                pending[qq].append((0, 0))
        if state["ready"] and (len(pending[q]) >= GROUP or left[q] == 0 or done > TAIL):
            flush(q)
        for item in list(waiting):
            if done >= item[0] + 3 and (item[1] < 2 or not todo):
                waiting.remove(item)
                settle(item[1])
        if left[q] == 0:
            exchange(q).start()
            waiting.append((done, q))
        remaining = len(RECEIVES) - done
        if todo:
            count = -(-len(todo) // max(1, remaining - 3))
            for start in todo[:count]:
                softmax_heads(start)
            del todo[:count]

    for start in todo:
        softmax_heads(start)
    sent = gathered.at[pl.ds(0, CHIPS - 1)]
    pltpu.make_async_remote_copy(
        src_ref=sent, dst_ref=sent, send_sem=gsend, recv_sem=trecv, device_id=sibling, device_id_type=MESH
    ).wait_send()
    all_feats(other).wait_send()
    for step in (1, 2, 3):
        raw_send(step).wait_send()
        spread(step).wait_send()
    for _, q in waiting:
        settle(q)
    for q in range(NQ):
        exchange(q).wait_send()


def finish_kernel(
    mixed, late_probs, late_values, gv, mv, attended, new_params, new_moment, late_mixed, early_sem, late_sem, p_sem, m_sem
):
    half = 2 * Q_GROUP * HD
    piece = Q_GROUP * HD
    early = pltpu.make_async_copy(mixed, attended.at[:, pl.ds((1 - LATE) * half, half)], early_sem)
    copies = [early, pltpu.make_async_copy(gv, new_params, p_sem), pltpu.make_async_copy(mv, new_moment, m_sem)]
    for copy in copies:
        copy.start()
    for j in range(2):
        values = late_values[:, j * HD : (j + 1) * HD]
        for i in range(Q_GROUP):
            h = j * Q_GROUP + i
            out = jnp.dot(late_probs[h], values, preferred_element_type=jnp.float32)
            late_mixed[:, h * HD : (h + 1) * HD] = out.astype(jnp.bfloat16)
        copy = pltpu.make_async_copy(
            late_mixed.at[:, pl.ds(j * piece, piece)],
            attended.at[:, pl.ds(LATE * half + j * piece, piece)],
            late_sem.at[j],
        )
        copy.start()
        copies.append(copy)
    for copy in copies:
        copy.wait()


def shards(tokens, queries, segments, local_weights, global_params, momentum):
    hbm = pl.BlockSpec(memory_space=pltpu.HBM)
    any_space = pl.BlockSpec(memory_space=pl.ANY)
    vmem = pl.BlockSpec(memory_space=pltpu.VMEM)
    dma = pltpu.SemaphoreType.DMA
    half = 2 * Q_GROUP
    kept = pl.pallas_call(
        kernel,
        out_shape=(
            pltpu.VMEM((ROWS, half * HD), jnp.bfloat16),
            pltpu.VMEM((half, ROWS, ROWS), jnp.bfloat16),
            pltpu.VMEM((ROWS, BLK), jnp.bfloat16),
            pltpu.VMEM((ROWS, KVW), jnp.float32),
            pltpu.VMEM((ROWS, KVW), jnp.float32),
        ),
        in_specs=[hbm, hbm, vmem, hbm, hbm, hbm],
        out_specs=(vmem,) * 5,
        scratch_shapes=[
            pltpu.VMEM((CHIPS, NQ, BLK, BLK), jnp.bfloat16),
            pltpu.VMEM((CHIPS, 2 * ROWS, BLK), jnp.bfloat16),
            pltpu.VMEM((NQ, 2 * ROWS, BLK), jnp.float32),
            pltpu.VMEM((NQ, ROWS, BLK), jnp.float32),
            pltpu.VMEM((ROWS, QH * HD), jnp.bfloat16),
            pltpu.VMEM((ROWS, ROWS), jnp.float32),
            pltpu.VMEM((half, ROWS, ROWS), jnp.bfloat16),
            pltpu.VMEM((ROWS, 2 * BLK), jnp.bfloat16),
            pltpu.VMEM((X, PART, KVW), jnp.bfloat16),
            pltpu.VMEM((PART, KVW), jnp.float32),
            pltpu.VMEM((PART, KVW), jnp.float32),
            pltpu.VMEM((X, PART, KVW), jnp.float32),
            dma, dma((NQ, 15)), dma, dma, dma((3,)), dma((3,)), dma, dma, dma((3,)), dma((3,)),
            dma((NQ,)), dma((NQ,)),
            dma((NQ,)), dma, dma, dma, dma, dma,
        ],
        compiler_params=pltpu.CompilerParams(
            collective_id=0, has_side_effects=True, vmem_limit_bytes=57 * 2**20
        ),
        cost_estimate=pl.CostEstimate(flops=6 * 10**9, bytes_accessed=13 * 2**20, transcendentals=2**21),
        name="sync_and_attend",
    )(tokens[0], queries[0], segments[0], local_weights[0], global_params, momentum)
    attended, new_params, new_momentum = pl.pallas_call(
        finish_kernel,
        out_shape=(
            jax.ShapeDtypeStruct((ROWS, QH * HD), jnp.bfloat16),
            jax.ShapeDtypeStruct((ROWS, KVW), jnp.float32),
            jax.ShapeDtypeStruct((ROWS, KVW), jnp.float32),
        ),
        in_specs=[vmem] * 5,
        out_specs=(any_space,) * 3,
        scratch_shapes=[pltpu.VMEM((ROWS, half * HD), jnp.bfloat16), dma, dma((2,)), dma, dma],
        compiler_params=pltpu.CompilerParams(vmem_limit_bytes=16 * 2**20),
        name="finish",
    )(*kept)
    return (attended[None], new_params, new_momentum)


def solution(mesh):
    placed = (
        P("replica", "fsdp", None),
        P("replica", "fsdp", None),
        P("replica", "fsdp", None),
        P("replica", "fsdp", None),
        P("fsdp", None),
        P("fsdp", None),
    )
    return jax.shard_map(
        shards,
        mesh=mesh,
        in_specs=placed,
        out_specs=(P("replica", "fsdp", None), P("fsdp", None), P("fsdp", None)),
        check_vma=False,
    )
```
